512 devices in a mesh: dp: 2 (over y_hi), seq: 32 (over y_lo, x, core), expert: 8 (over z).
Axes of the slice: x: 4, y: 8 (y_hi: 2, y_lo: 4; y = y_hi * 4 + y_lo), z: 8, core: 2. Of those that a mesh axis runs over, the one named last changes fastest.
Arguments:
- tokens: bfloat16 [2, 24576, 1280], P('dp', 'seq'), may hold values from -36 to 36
- slot_weight: bfloat16 [1024, 1280], P(('seq', 'expert')), may hold values from -1.5 to 1.5
- slot_output: bfloat16 [2, 1024, 1280], P('dp', ('seq', 'expert')), may hold values from -6 to 6
- slot_input_grad: bfloat16 [2, 1024, 1280], P('dp', ('seq', 'expert')), may hold values from -0.59765625 to 0.59765625
- output_grad: bfloat16 [2, 24576, 1280], P('dp', 'seq'), may hold values from -1.1953125 to 1.1953125
Outputs:
- token_grad: bfloat16 [2, 24576, 1280], P('dp', ('seq', 'expert'))
- slot_output_grad: bfloat16 [2, 1024, 1280], P('dp', ('seq', 'expert'))
- slot_weight_grad: float32 [1024, 1280], P(('seq', 'expert'))
The draws below stay inside these ranges and needn't reach their ends.
All inputs are finite; a program needn't handle non-finite values.
Results may differ from the reference program's by a relative error of at most 0.015.
Values may be sent and summed in bfloat16 or wider, within the bound.
A program may use at most 64 MiB of HBM per device.

```python
import math
import jax
import jax.numpy as jnp
from jax import lax

D = 1280
EXP_DEV = 4
EXPERTS = 1024
SEQ_LEN = 24576
BATCH = 2
N_SEQ = 32
N_EXPERT = 8


def planted_parts(key):
    sign_key, expert_key, place_key, offset_key = jax.random.split(key, 4)
    sign_vector = jnp.where(jax.random.bernoulli(sign_key, 0.5, (D,)), 1.0, -1.0).astype(jnp.float32)
    first_expert = jax.random.randint(expert_key, (), 0, EXPERTS)
    second_expert = (first_expert + jax.random.randint(offset_key, (), 1, EXPERTS)) % EXPERTS
    places = jax.random.randint(place_key, (BATCH, 6), 0, SEQ_LEN)
    return (sign_vector, first_expert, second_expert, places)


def draw_tokens(key, part):
    sign_vector, first_expert, second_expert, places = planted_parts(key)
    key = jax.random.fold_in(key, 11)
    scale_key, value_key = jax.random.split(key, 2)
    position = jnp.arange(SEQ_LEN, dtype=jnp.float32)[None, :, None]
    spread = jnp.exp(jax.random.uniform(scale_key, (BATCH, SEQ_LEN, 1), minval=math.log(0.3), maxval=math.log(3.0)))
    position_ramp = 1.0 + 2.0 * position / SEQ_LEN
    noise_part = jnp.clip(jax.random.normal(value_key, (BATCH, SEQ_LEN, D)), -4.0, 4.0)
    values = spread * position_ramp * noise_part
    strengths = [4.0, 4.0625, 5.5, 5.5625, 7.0, 7.0625]
    token_index = jnp.arange(SEQ_LEN)[None, :]
    for planted in range(6):
        planted_row = (token_index == places[:, planted:planted + 1])[:, :, None]
        values = jnp.where(planted_row, strengths[planted] * sign_vector[None, None, :], values)
    return values.astype(jnp.float32).astype(jnp.bfloat16)


def draw_slot_weight(key, part):
    sign_vector, first_expert, second_expert, places = planted_parts(key)
    key = jax.random.fold_in(key, 23)
    scale_key, value_key = jax.random.split(key, 2)
    column_scale = jnp.exp(jax.random.uniform(scale_key, (EXPERTS, 1), minval=math.log(0.3), maxval=math.log(3.0)))
    noise_part = jnp.clip(jax.random.normal(value_key, (EXPERTS, D)), -4.0, 4.0)
    values = noise_part * column_scale / math.sqrt(D)
    expert_index = jnp.arange(EXPERTS)[:, None]
    feature_index = jnp.arange(D)[None, :]
    halved_count = max(2, 24 * D // 1280)
    planted_first = sign_vector[None, :] * (32.0 / D)
    planted_second = jnp.where(feature_index < halved_count, 0.5 * planted_first, planted_first)
    values = jnp.where(expert_index == first_expert, planted_first, values)
    values = jnp.where(expert_index == second_expert, planted_second, values)
    return values.astype(jnp.float32).astype(jnp.bfloat16)


def levels(own_key, shape, cuts, smallest, largest):
    factor_of = 1.0
    for dim, blocks in cuts:
        draws = jax.random.uniform(jax.random.fold_in(jax.random.fold_in(own_key, 6), dim), (blocks,), jnp.float32, smallest / len(cuts), largest / len(cuts))
        factor_of = factor_of * jnp.repeat(jnp.exp(draws), shape[dim] // blocks).reshape((-1,) + (1,) * (len(shape) - 1 - dim))
    return factor_of


def gaussian(rng, dims, deviation, reach, pieces=(), held_as=jnp.bfloat16):
    gain = levels(rng, dims, pieces, -0.22, 0.18) if pieces else 1.0
    array = jax.random.normal(rng, dims, jnp.float32) * deviation * gain
    return jnp.minimum(jnp.maximum(array, -reach), reach).astype(held_as)


def setup_inputs(seed: int = 0) -> dict:
    streams_of = jax.random.split(jax.random.key(seed), 6)
    tokens = draw_tokens(jax.random.fold_in(streams_of[5], 71), 0)
    slot_weight = draw_slot_weight(jax.random.fold_in(streams_of[5], 71), 0)
    slot_output = gaussian(streams_of[2], (BATCH, EXPERTS, D), 1.0, 6.0, ((0, 2), (1, 256)))
    slot_input_grad = gaussian(streams_of[3], (BATCH, EXPERTS, D), 0.1, 0.59765625, ((0, 2), (1, 256)))
    output_grad = gaussian(streams_of[4], (BATCH, SEQ_LEN, D), 0.2, 1.1953125, ((0, 2), (1, 32)))
    return {"tokens": tokens, "slot_weight": slot_weight, "slot_output": slot_output, "slot_input_grad": slot_input_grad, "output_grad": output_grad}


def reference(tokens, slot_weight, slot_output, slot_input_grad, output_grad):
    token_list = []
    slot_list = []
    weight_total = jnp.zeros((EXPERTS, D), jnp.float32)
    phi_groups = slot_weight.reshape(N_SEQ, N_EXPERT, EXP_DEV, D)
    for batch_row in range(BATCH):
        token_rows = tokens[batch_row]
        grad_rows = output_grad[batch_row]
        outputs_here = slot_output[batch_row]
        inputs_grad = slot_input_grad[batch_row]
        logits = jnp.dot(token_rows, slot_weight.T, preferred_element_type=jnp.float32)
        column_peak = jnp.max(logits, axis=0, keepdims=True)
        column_exp = jnp.exp(logits - column_peak)
        dispatch = column_exp / jnp.sum(column_exp, axis=0, keepdims=True)
        row_peak = jnp.max(logits, axis=1, keepdims=True)
        row_exp = jnp.exp(logits - row_peak)
        combine = row_exp / jnp.sum(row_exp, axis=1, keepdims=True)
        combine_grad = jnp.dot(grad_rows, outputs_here.T, preferred_element_type=jnp.float32)
        dispatch_grad = jnp.dot(token_rows, inputs_grad.T, preferred_element_type=jnp.float32)
        row_dot = jnp.sum(combine * combine_grad, axis=1, keepdims=True)
        column_dot = jnp.sum(dispatch * dispatch_grad, axis=0, keepdims=True)
        logit_grad = combine * (combine_grad - row_dot) + dispatch * (dispatch_grad - column_dot)
        logit_half = logit_grad.astype(jnp.bfloat16)
        dispatch_half = dispatch.astype(jnp.bfloat16)
        combine_half = combine.astype(jnp.bfloat16)
        slot_list.append(jnp.dot(combine_half.T, grad_rows, preferred_element_type=jnp.float32).astype(jnp.bfloat16))
        weight_total = weight_total + jnp.dot(logit_grad.T, token_rows.astype(jnp.float32), precision=lax.Precision.HIGHEST, preferred_element_type=jnp.float32)
        length = token_rows.shape[0]
        dispatch_groups = dispatch_half.reshape(length, N_SEQ, N_EXPERT, EXP_DEV)
        logit_groups = logit_half.reshape(length, N_SEQ, N_EXPERT, EXP_DEV)
        input_groups = inputs_grad.reshape(N_SEQ, N_EXPERT, EXP_DEV, D)
        token_total = jnp.zeros((length, D), jnp.float32)
        for group in range(N_EXPERT):
            left_side = jnp.concatenate([dispatch_groups[:, :, group, :].reshape(length, N_SEQ * EXP_DEV), logit_groups[:, :, group, :].reshape(length, N_SEQ * EXP_DEV)], axis=1)
            right_side = jnp.concatenate([input_groups[:, group].reshape(N_SEQ * EXP_DEV, D), phi_groups[:, group].reshape(N_SEQ * EXP_DEV, D)], axis=0)
            group_term = lax.optimization_barrier(jnp.dot(left_side, right_side, preferred_element_type=jnp.float32).astype(jnp.bfloat16))
            token_total = token_total + group_term.astype(jnp.float32)
        token_list.append(token_total.astype(jnp.bfloat16))
    return (jnp.stack(token_list, 0), jnp.stack(slot_list, 0), weight_total)
```

```python
import jax
import jax.numpy as jnp
from jax import lax
from jax.experimental import pallas as pl
from jax.experimental.pallas import tpu as pltpu
from jax.sharding import PartitionSpec as P

F32 = jnp.float32
BF16 = jnp.bfloat16
MESH = pl.DeviceIdType.MESH

NY, NX, NC, NZ = 4, 4, 2, 8
NSEQ = NY * NX * NC
D = 1280
TOK = 768
EXP = 128
OWN = TOK // NZ
HALF = OWN // 2

RIGHT = ((4, 0), (3, 1), (3, 0), (2, 1), (2, 0), (1, 1), (1, 0))
LEFT = ((4, 1), (3, 0), (3, 1), (2, 0), (2, 1), (1, 0), (1, 1))


def nt_dot(a, b):
    return lax.dot_general(a, b, (((1,), (1,)), ((), ())), preferred_element_type=F32)


def nn_dot(a, b):
    return jnp.dot(a, b, preferred_element_type=F32)


def kernel(
    tok_hbm, phi_ref, out_ref, inp_ref, og_hbm,
    tg_ref, so_ref, sw_ref,
    tok, og, shard, params, logit, cgrad, dgrad, row_exp, col_exp, col_tile, row_stat, col_stat,
    mat, comb, fac, part, stage, ring_in,
    w_sum, o_sum, w_core, o_core, w_x, o_x, w_xin, o_xin, y_out, y_in, dp_out, dp_in,
    load_sem, ys, yr, xs, xr, cs, cr, stat_s, stat_r, ring_s, ring_r, rc_s, rc_r, rx_s, rx_r, ry_s, ry_r, dp_s, dp_r,
):
    dp = lax.axis_index("dp")
    seq = lax.axis_index("seq")
    z = lax.axis_index("expert")
    core = lax.rem(seq, NC)
    x = lax.rem(seq // NC, NX)
    y = seq // (NC * NX)

    def seq_of(yy, xx, cc):
        return (yy * NX + xx) * NC + cc

    load_tok = pltpu.make_async_copy(tok_hbm, tok, load_sem.at[0])
    load_og = pltpu.make_async_copy(og_hbm, og, load_sem.at[1])
    load_tok.start()
    load_og.start()
    shard[y, 0] = phi_ref[...]
    shard[y, 1] = inp_ref[...]
    shard[y, 2] = out_ref[...]

    barrier = pltpu.get_barrier_semaphore()

    @pl.loop(1, NSEQ)
    def _(j):
        pl.semaphore_signal(
            barrier, inc=1, device_id={"seq": lax.rem(seq + j, NSEQ)}, device_id_type=MESH
        )

    @pl.loop(1, NZ)
    def _(j):
        pl.semaphore_signal(
            barrier, inc=1, device_id={"expert": lax.rem(z + j, NZ)}, device_id_type=MESH
        )

    pl.semaphore_signal(barrier, inc=1, device_id={"dp": 1 - dp}, device_id_type=MESH)
    pl.semaphore_wait(barrier, NSEQ + NZ - 1)

    pending = []

    def send(src, dst, s_sem, r_sem, device):
        copy = pltpu.make_async_remote_copy(
            src_ref=src, dst_ref=dst, send_sem=s_sem, recv_sem=r_sem,
            device_id=device, device_id_type=MESH,
        )
        copy.start()
        pending.append(copy)
        return copy

    y_copies = [
        send(
            shard.at[y], shard.at[y], ys.at[j - 1], yr.at[j - 1],
            {"seq": seq_of(lax.rem(y + j, NY), x, core)},
        )
        for j in range(1, NY)
    ]
    for copy in y_copies:
        copy.wait_recv()
    for t in range(3):
        rows = [shard[j, t].astype(F32) for j in range(NY)]
        params[t, core, x] = jnp.concatenate(rows, axis=0).astype(BF16)
    sibling = {"seq": seq_of(y, x, 1 - core)}
    own_block = params.at[:, core, x]
    x_copies = [
        send(
            own_block, own_block, xs.at[j - 1], xr.at[j - 1],
            {"seq": seq_of(y, lax.rem(x + j, NX), core)},
        )
        for j in range(1, NX)
    ]
    c_copies = [send(own_block, own_block, cs.at[0], cr.at[0], sibling)]
    for j in (1, 3, 2):
        x_copies[j - 1].wait_recv()
        block = params.at[:, core, lax.rem(x - j + NX, NX)]
        c_copies.append(send(block, block, cs.at[j], cr.at[j], sibling))
    load_tok.wait()
    load_og.wait()
    for copy in c_copies:
        copy.wait_recv()

    both = params[0:2].reshape(2 * EXP, D)
    outs = params[2].reshape(EXP, D)
    for n in range(TOK // 256):
        cols = slice(256 * n, 256 * (n + 1))
        pair = nt_dot(both, tok[cols, :])
        logit[:, cols] = pair[:EXP]
        dgrad[:, cols] = pair[EXP:]
        cgrad[:, cols] = nt_dot(outs, og[cols, :])

    ROWS = 16
    blocks = [slice(ROWS * b, ROWS * (b + 1)) for b in range(EXP // ROWS)]
    top = logit[blocks[0], :]
    for rows in blocks[1:]:
        top = jnp.maximum(top, logit[rows, :])
    row_max = jnp.max(top, axis=0, keepdims=True)
    row_sum = jnp.zeros((ROWS, TOK), F32)
    row_dot = jnp.zeros((ROWS, TOK), F32)
    lane = lax.broadcasted_iota(jnp.int32, (ROWS, EXP), 1)
    for rows in blocks:
        value = logit[rows, :]
        by_row = jnp.exp(value - row_max)
        row_exp[rows, :] = by_row
        row_sum = row_sum + by_row
        row_dot = row_dot + by_row * cgrad[rows, :]
        col_max = jnp.max(value, axis=1, keepdims=True)
        by_col = jnp.exp(value - col_max)
        col_exp[rows, :] = by_col
        col_sum = jnp.sum(by_col, axis=1, keepdims=True)
        col_dot = jnp.sum(by_col * dgrad[rows, :], axis=1, keepdims=True)
        col_tile[rows, :] = jnp.where(
            lane == 0, col_max, jnp.where(lane == 1, col_sum, jnp.where(lane == 2, col_dot, 0.0))
        )
    row_stat[z] = jnp.concatenate(
        [
            row_max,
            jnp.sum(row_sum, axis=0, keepdims=True),
            jnp.sum(row_dot, axis=0, keepdims=True),
            jnp.zeros((1, TOK), F32),
        ],
        axis=0,
    )
    col_stat[seq] = col_tile[...].T[0:4, :]

    @pl.loop(1, NZ)
    def _(j):
        pltpu.make_async_remote_copy(
            src_ref=row_stat.at[z], dst_ref=row_stat.at[z],
            send_sem=stat_s.at[0], recv_sem=stat_r.at[0],
            device_id={"expert": lax.rem(z + j, NZ)}, device_id_type=MESH,
        ).start()

    @pl.loop(1, NSEQ)
    def _(j):
        pltpu.make_async_remote_copy(
            src_ref=col_stat.at[seq], dst_ref=col_stat.at[seq],
            send_sem=stat_s.at[1], recv_sem=stat_r.at[1],
            device_id={"seq": lax.rem(seq + j, NSEQ)}, device_id_type=MESH,
        ).start()

    row_all = row_stat.at[pl.ds(0, NZ - 1)]
    col_all = col_stat.at[pl.ds(0, NSEQ - 1)]
    pltpu.make_async_copy(row_all, row_all, stat_r.at[0]).wait()

    def join(stat, count):
        best = stat[0][0:1]
        for j in range(1, count):
            best = jnp.maximum(best, stat[j][0:1])
        total = jnp.zeros(stat.shape[1:], F32)
        for j in range(count):
            one = stat[j]
            total = total + jnp.exp(one[0:1] - best) * one
        return best, total[1:2], total[2:3]

    best, mass, dot = join(row_stat, NZ)
    row_scale = jnp.exp(row_stat[z][0:1] - best) / mass
    row_mean = dot / mass
    pltpu.make_async_copy(col_all, col_all, stat_r.at[1]).wait()
    best, mass, dot = join(col_stat, NSEQ)
    lines = lax.broadcasted_iota(jnp.int32, (EXP, EXP), 0)
    col_tile[...] = jnp.where(
        lines == 0,
        jnp.exp(col_stat[seq][0:1] - best) / mass,
        jnp.where(lines == 1, dot / mass, 0.0),
    ).T

    for b, rows in enumerate(blocks):
        combine = row_exp[rows, :] * row_scale
        dispatch = col_exp[rows, :] * col_tile[rows, 0:1]
        grad = combine * (cgrad[rows, :] - row_mean) + dispatch * (dgrad[rows, :] - col_tile[rows, 1:2])
        high = grad.astype(BF16)
        mat[rows, :] = (grad - high.astype(F32)).astype(BF16)
        mat[EXP + ROWS * b:EXP + ROWS * (b + 1), :] = high
        mat[2 * EXP + ROWS * b:2 * EXP + ROWS * (b + 1), :] = dispatch.astype(BF16)
        comb[rows, :] = combine.astype(BF16)
    fac[...] = mat[EXP:3 * EXP, :].T

    def term(d):
        stacked = params[0:2].reshape(2 * EXP, D)
        owner = lax.rem(z + d, NZ)
        part[d] = nn_dot(fac[pl.ds(pl.multiple_of(owner * OWN, OWN), OWN), :], stacked)

    ring = ({}, {})
    towards = ({"expert": lax.rem(z + 1, NZ)}, {"expert": lax.rem(z + NZ - 1, NZ)})

    def pass_on(way, i):
        d, h = (RIGHT, LEFT)[way][i]
        value = part[d if way == 0 else NZ - d, HALF * h:HALF * (h + 1), :]
        if (d + 1, h) in ring[way]:
            j, copy = ring[way][(d + 1, h)]
            copy.wait_recv()
            value = value + ring_in[way, j].astype(F32)
        stage[way, i] = value.astype(BF16)
        ring[way][(d, h)] = (
            i,
            send(stage.at[way, i], ring_in.at[way, i], ring_s.at[way, i], ring_r.at[way, i], towards[way]),
        )

    term(4)
    pass_on(0, 0)
    pass_on(1, 0)
    term(3)
    pass_on(0, 1)
    term(5)
    pass_on(1, 1)

    for n in range(D // 256):
        cols = slice(256 * n, 256 * (n + 1))
        pair = nn_dot(mat[0:2 * EXP, :], tok[:, cols])
        w_sum[:, cols] = pair[:EXP] + pair[EXP:]
        o_sum[:, cols] = nn_dot(comb[...], og[:, cols]).astype(BF16)
    there = pl.ds(pl.multiple_of((1 - core) * (EXP // 2), EXP // 2), EXP // 2)
    here = pl.ds(pl.multiple_of(core * (EXP // 2), EXP // 2), EXP // 2)
    core_w = send(w_sum.at[there], w_core, rc_s.at[0], rc_r.at[0], sibling)
    core_o = send(o_sum.at[there], o_core, rc_s.at[1], rc_r.at[1], sibling)
    for d in (2, 6, 1, 7, 0):
        term(d)

    pass_on(0, 2)
    pass_on(1, 2)

    core_w.wait_recv()
    core_o.wait_recv()
    w_x[...] = (w_sum[here, :] + w_core[...]).reshape(NX, 16, D)
    o_x[...] = (o_sum[here, :].astype(F32) + o_core[...].astype(F32)).astype(BF16).reshape(NX, 16, D)
    x_sums = []
    for j in range(1, NX):
        to = lax.rem(x + j, NX)
        device = {"seq": seq_of(y, to, core)}
        x_sums.append(send(w_x.at[to], w_xin.at[j - 1], rx_s.at[0, j - 1], rx_r.at[0, j - 1], device))
        x_sums.append(send(o_x.at[to], o_xin.at[j - 1], rx_s.at[1, j - 1], rx_r.at[1, j - 1], device))

    pass_on(0, 3)
    pass_on(1, 3)
    pass_on(0, 4)
    pass_on(1, 4)

    for copy in x_sums:
        copy.wait_recv()
    w16 = w_x[x]
    o16 = o_x[x].astype(F32)
    for j in range(NX - 1):
        w16 = w16 + w_xin[j]
        o16 = o16 + o_xin[j].astype(F32)
    for j in range(NY):
        y_out[j, 0:4] = w16[4 * j:4 * j + 4]
        y_out[j, 4:8] = o16[4 * j:4 * j + 4]
    y_sums = []
    for j in range(1, NY):
        to = lax.rem(y + j, NY)
        y_sums.append(
            send(y_out.at[to], y_in.at[j - 1], ry_s.at[j - 1], ry_r.at[j - 1], {"seq": seq_of(to, x, core)})
        )

    pass_on(0, 5)
    pass_on(1, 5)

    for copy in y_sums:
        copy.wait_recv()
    total = y_out[y]
    for j in range(NY - 1):
        total = total + y_in[j]
    dp_out[...] = total
    dp_copy = send(dp_out, dp_in, dp_s, dp_r, {"dp": 1 - dp})
    so_ref[...] = total[4:8].astype(BF16)

    pass_on(0, 6)
    pass_on(1, 6)

    dp_copy.wait_recv()
    sw_ref[...] = dp_out[0:4] + dp_in[0:4]

    for h in (1, 0):
        value = part[0, HALF * h:HALF * (h + 1), :]
        for way in range(2):
            j, copy = ring[way][(1, h)]
            copy.wait_recv()
            value = value + ring_in[way, j].astype(F32)
        tg_ref[HALF * h:HALF * (h + 1), :] = value.astype(BF16)

    for copy in pending:
        copy.wait_send()
    pltpu.make_async_copy(row_all, row_all, stat_s.at[0]).wait()
    pltpu.make_async_copy(col_all, col_all, stat_s.at[1]).wait()


def on_device(tokens, slot_weight, slot_output, slot_input_grad, output_grad):
    vmem = pl.BlockSpec(memory_space=pltpu.VMEM)
    hbm = pl.BlockSpec(memory_space=pl.ANY)
    dma = pltpu.SemaphoreType.DMA
    token_grad, slot_output_grad, slot_weight_grad = pl.pallas_call(
        kernel,
        out_shape=(
            jax.ShapeDtypeStruct((OWN, D), BF16),
            jax.ShapeDtypeStruct((4, D), BF16),
            jax.ShapeDtypeStruct((4, D), F32),
        ),
        in_specs=[hbm, vmem, vmem, vmem, hbm],
        out_specs=(vmem, vmem, vmem),
        scratch_shapes=[
            pltpu.VMEM((TOK, D), BF16),
            pltpu.VMEM((TOK, D), BF16),
            pltpu.VMEM((NY, 3, 4, D), BF16),
            pltpu.VMEM((3, NC, NX, 16, D), BF16),
            pltpu.VMEM((EXP, TOK), F32),
            pltpu.VMEM((EXP, TOK), F32),
            pltpu.VMEM((EXP, TOK), F32),
            pltpu.VMEM((EXP, TOK), F32),
            pltpu.VMEM((EXP, TOK), F32),
            pltpu.VMEM((EXP, EXP), F32),
            pltpu.VMEM((NZ, 4, TOK), F32),
            pltpu.VMEM((NSEQ, 4, EXP), F32),
            pltpu.VMEM((3 * EXP, TOK), BF16),
            pltpu.VMEM((EXP, TOK), BF16),
            pltpu.VMEM((TOK, 2 * EXP), BF16),
            pltpu.VMEM((NZ, OWN, D), F32),
            pltpu.VMEM((2, 7, HALF, D), BF16),
            pltpu.VMEM((2, 7, HALF, D), BF16),
            pltpu.VMEM((EXP, D), F32),
            pltpu.VMEM((EXP, D), BF16),
            pltpu.VMEM((EXP // 2, D), F32),
            pltpu.VMEM((EXP // 2, D), BF16),
            pltpu.VMEM((NX, 16, D), F32),
            pltpu.VMEM((NX, 16, D), BF16),
            pltpu.VMEM((NX - 1, 16, D), F32),
            pltpu.VMEM((NX - 1, 16, D), BF16),
            pltpu.VMEM((NY, 8, D), F32),
            pltpu.VMEM((NY - 1, 8, D), F32),
            pltpu.VMEM((8, D), F32),
            pltpu.VMEM((8, D), F32),
            dma((2,)),
            dma((3,)), dma((3,)),
            dma((3,)), dma((3,)),
            dma((4,)), dma((4,)),
            dma((2,)), dma((2,)),
            dma((2, 7)), dma((2, 7)),
            dma((2,)), dma((2,)),
            dma((2, 3)), dma((2, 3)),
            dma((3,)), dma((3,)),
            dma(()), dma(()),
        ],
        compiler_params=pltpu.CompilerParams(
            collective_id=0, has_side_effects=True, vmem_limit_bytes=50 * 1024 * 1024
        ),
        cost_estimate=pl.CostEstimate(
            flops=2_000_000_000, bytes_accessed=5_000_000, transcendentals=250_000
        ),
    )(tokens[0], slot_weight, slot_output[0], slot_input_grad[0], output_grad[0])
    return (token_grad[None], slot_output_grad[None], slot_weight_grad)


def solution(mesh):
    placed = (
        P("dp", "seq", None),
        P(("seq", "expert"), None),
        P("dp", ("seq", "expert"), None),
        P("dp", ("seq", "expert"), None),
        P("dp", "seq", None),
    )
    return jax.shard_map(
        on_device,
        mesh=mesh,
        in_specs=placed,
        out_specs=(
            P("dp", ("seq", "expert"), None),
            P("dp", ("seq", "expert"), None),
            P(("seq", "expert"), None),
        ),
        check_vma=False,
    )
```

```python
import jax
import jax.numpy as jnp
from jax import lax
from jax.experimental import pallas as pl
from jax.experimental.pallas import tpu as pltpu
from jax.sharding import PartitionSpec as P

F32 = jnp.float32
BF16 = jnp.bfloat16
MESH = pl.DeviceIdType.MESH

NY, NX, NC, NZ = 4, 4, 2, 8
NSEQ = NY * NX * NC
D = 1280
TOK = 768
EXP = 128
OWN = TOK // NZ
HALF = OWN // 2

RIGHT = ((4, 0), (3, 1), (3, 0), (2, 1), (2, 0), (1, 1), (1, 0))
LEFT = ((4, 1), (3, 0), (3, 1), (2, 0), (2, 1), (1, 0), (1, 1))


def nt_dot(a, b):
    return lax.dot_general(a, b, (((1,), (1,)), ((), ())), preferred_element_type=F32)


def nn_dot(a, b):
    return jnp.dot(a, b, preferred_element_type=F32)


def kernel(
    tok_hbm, phi_hbm, out_hbm, inp_hbm, og_hbm,
    tg_ref, so_ref, sw_ref,
    tok, og, shard, params, logit, cgrad, dgrad, row_exp, col_exp, col_tile, row_stat, col_stat,
    mat, comb, fac, part, stage, ring_in,
    w_sum, o_sum, w_core, o_core, w_mid, o_mid, w_min, o_min, w_end, o_end, w_ein, o_ein,
    load_sem, ys, yr, xs, xr, cs, cr, stat_s, stat_r, ring_s, ring_r, rc_s, rc_r, rm_s, rm_r, re_s, re_r,
):
    dp = lax.axis_index("dp")
    seq = lax.axis_index("seq")
    z = lax.axis_index("expert")
    core = lax.rem(seq, NC)
    x = lax.rem(seq // NC, NX)
    y = seq // (NC * NX)

    a = jnp.where(core == 0, y, x)
    b = jnp.where(core == 0, x, y)

    def seq_of(aa, bb):
        yy = jnp.where(core == 0, aa, bb)
        xx = jnp.where(core == 0, bb, aa)
        return (yy * NX + xx) * NC + core

    barrier = pltpu.get_barrier_semaphore()

    def greet(device):
        pl.semaphore_signal(barrier, inc=1, device_id=device, device_id_type=MESH)

    @pl.loop(1, NSEQ)
    def _(j):
        greet({"seq": lax.rem(seq + j, NSEQ)})

    @pl.loop(1, NZ)
    def _(j):
        greet({"expert": lax.rem(z + j, NZ)})

    for j in range(NY):
        greet({"dp": 1 - dp, "seq": seq_of(lax.rem(a + j, NY), b)})

    small = (phi_hbm, inp_hbm, out_hbm)
    load_small = [
        pltpu.make_async_copy(src, shard.at[a, t], load_sem.at[2 + t]) for t, src in enumerate(small)
    ]
    for copy in load_small:
        copy.start()
    load_tok = pltpu.make_async_copy(tok_hbm, tok, load_sem.at[0])
    load_og = pltpu.make_async_copy(og_hbm, og, load_sem.at[1])
    load_tok.start()
    load_og.start()
    pl.semaphore_wait(barrier, NSEQ + NZ - 2 + NY)

    pending = []

    def send(src, dst, s_sem, r_sem, device):
        copy = pltpu.make_async_remote_copy(
            src_ref=src, dst_ref=dst, send_sem=s_sem, recv_sem=r_sem,
            device_id=device, device_id_type=MESH,
        )
        copy.start()
        pending.append(copy)
        return copy

    y_copies = [
        [
            send(
                src, shard.at[a, t], ys.at[j - 1, t], yr.at[j - 1, t],
                {"seq": seq_of(lax.rem(a + j, NY), b)},
            )
            for t, src in enumerate(small)
        ]
        for j in range(1, NY)
    ]
    for copy in load_small:
        copy.wait()
    for copies in y_copies:
        for copy in copies:
            copy.wait_recv()
    for t in range(3):
        rows = [shard[j, t].astype(F32) for j in range(NY)]
        params[t, core, b] = jnp.concatenate(rows, axis=0).astype(BF16)
    sibling = {"seq": seq + 1 - 2 * core}
    own_block = params.at[:, core, b]
    x_copies = [
        send(
            own_block, own_block, xs.at[j - 1], xr.at[j - 1],
            {"seq": seq_of(a, lax.rem(b + j, NX))},
        )
        for j in range(1, NX)
    ]
    c_copies = [send(own_block, own_block, cs.at[0], cr.at[0], sibling)]
    for j in (1, 3, 2):
        x_copies[j - 1].wait_recv()
        block = params.at[:, core, lax.rem(b - j + NX, NX)]
        c_copies.append(send(block, block, cs.at[j], cr.at[j], sibling))
    load_tok.wait()
    load_og.wait()
    for copy in c_copies:
        copy.wait_recv()

    both = params[0:2].reshape(2 * EXP, D)
    outs = params[2].reshape(EXP, D)
    for n in range(TOK // 256):
        cols = slice(256 * n, 256 * (n + 1))
        pair = nt_dot(both, tok[cols, :])
        logit[:, cols] = pair[:EXP]
        dgrad[:, cols] = pair[EXP:]
        cgrad[:, cols] = nt_dot(outs, og[cols, :])

    ROWS = 16
    blocks = [slice(ROWS * b, ROWS * (b + 1)) for b in range(EXP // ROWS)]
    top = logit[blocks[0], :]
    for rows in blocks[1:]:
        top = jnp.maximum(top, logit[rows, :])
    row_max = jnp.max(top, axis=0, keepdims=True)
    row_sum = jnp.zeros((ROWS, TOK), F32)
    row_dot = jnp.zeros((ROWS, TOK), F32)
    lane = lax.broadcasted_iota(jnp.int32, (ROWS, EXP), 1)
    for rows in blocks:
        value = logit[rows, :]
        by_row = jnp.exp(value - row_max)
        row_exp[rows, :] = by_row
        row_sum = row_sum + by_row
        row_dot = row_dot + by_row * cgrad[rows, :]
        col_max = jnp.max(value, axis=1, keepdims=True)
        by_col = jnp.exp(value - col_max)
        col_exp[rows, :] = by_col
        col_sum = jnp.sum(by_col, axis=1, keepdims=True)
        col_dot = jnp.sum(by_col * dgrad[rows, :], axis=1, keepdims=True)
        col_tile[rows, :] = jnp.where(
            lane == 0,
            col_max + jnp.log(col_sum),
            jnp.where(lane == 1, col_dot / col_sum, jnp.where(lane == 2, col_max, 0.0)),
        )
    row_sum = jnp.sum(row_sum, axis=0, keepdims=True)
    row_dot = jnp.sum(row_dot, axis=0, keepdims=True)
    row_stat[z] = jnp.concatenate([row_max + jnp.log(row_sum), row_dot / row_sum], axis=0)
    turned = col_tile[...].T
    col_stat[seq] = turned[0:2, :]
    col_top = turned[2:3, :]
    @pl.loop(1, NZ)
    def _(j):
        pltpu.make_async_remote_copy(
            src_ref=row_stat.at[z], dst_ref=row_stat.at[z],
            send_sem=stat_s.at[0], recv_sem=stat_r.at[0],
            device_id={"expert": lax.rem(z + j, NZ)}, device_id_type=MESH,
        ).start()

    @pl.loop(1, NSEQ)
    def _(j):
        pltpu.make_async_remote_copy(
            src_ref=col_stat.at[seq], dst_ref=col_stat.at[seq],
            send_sem=stat_s.at[1], recv_sem=stat_r.at[1],
            device_id={"seq": lax.rem(seq + j, NSEQ)}, device_id_type=MESH,
        ).start()

    row_all = row_stat.at[pl.ds(0, NZ - 1)]
    col_all = col_stat.at[pl.ds(0, NSEQ - 1)]
    pltpu.make_async_copy(row_all, row_all, stat_r.at[0]).wait()

    def join(stat, count):
        best = stat[0][0:1]
        for j in range(1, count):
            best = jnp.maximum(best, stat[j][0:1])
        mass = jnp.zeros_like(best)
        mean = jnp.zeros_like(best)
        for j in range(count):
            one = stat[j]
            weight = jnp.exp(one[0:1] - best)
            mass = mass + weight
            mean = mean + weight * one[1:2]
        return best, mass, mean / mass

    best, mass, row_mean = join(row_stat, NZ)
    row_scale = jnp.exp(row_max - best) / mass
    pltpu.make_async_copy(col_all, col_all, stat_r.at[1]).wait()
    best, mass, col_mean = join(col_stat, NSEQ)
    lines = lax.broadcasted_iota(jnp.int32, (EXP, EXP), 0)
    col_tile[...] = jnp.where(
        lines == 0, jnp.exp(col_top - best) / mass, jnp.where(lines == 1, col_mean, 0.0)
    ).T

    for n, rows in enumerate(blocks):
        combine = row_exp[rows, :] * row_scale
        dispatch = col_exp[rows, :] * col_tile[rows, 0:1]
        grad = combine * (cgrad[rows, :] - row_mean) + dispatch * (dgrad[rows, :] - col_tile[rows, 1:2])
        high = grad.astype(BF16)
        mat[rows, :] = (grad - high.astype(F32)).astype(BF16)
        mat[EXP + ROWS * n:EXP + ROWS * (n + 1), :] = high
        mat[2 * EXP + ROWS * n:2 * EXP + ROWS * (n + 1), :] = dispatch.astype(BF16)
        comb[rows, :] = combine.astype(BF16)
    fac[...] = mat[EXP:3 * EXP, :].T

    def term(d):
        stacked = params[0:2].reshape(2 * EXP, D)
        owner = lax.rem(z + d, NZ)
        part[d] = nn_dot(fac[pl.ds(pl.multiple_of(owner * OWN, OWN), OWN), :], stacked)

    ring = ({}, {})
    towards = ({"expert": lax.rem(z + 1, NZ)}, {"expert": lax.rem(z + NZ - 1, NZ)})

    def pass_on(way, i):
        d, h = (RIGHT, LEFT)[way][i]
        value = part[d if way == 0 else NZ - d, HALF * h:HALF * (h + 1), :]
        if (d + 1, h) in ring[way]:
            j, copy = ring[way][(d + 1, h)]
            copy.wait_recv()
            value = value + ring_in[way, j].astype(F32)
        stage[way, i] = value.astype(BF16)
        ring[way][(d, h)] = (
            i,
            send(stage.at[way, i], ring_in.at[way, i], ring_s.at[way, i], ring_r.at[way, i], towards[way]),
        )

    term(4)
    pass_on(0, 0)
    pass_on(1, 0)
    term(3)
    pass_on(0, 1)
    term(5)
    pass_on(1, 1)

    for n in range(D // 256):
        cols = slice(256 * n, 256 * (n + 1))
        pair = nn_dot(mat[0:2 * EXP, :], tok[:, cols])
        w_sum[:, cols] = pair[:EXP] + pair[EXP:]
        o_sum[:, cols] = nn_dot(comb[...], og[:, cols]).astype(BF16)
    there = pl.ds(pl.multiple_of((1 - core) * (EXP // 2), EXP // 2), EXP // 2)
    here = pl.ds(pl.multiple_of(core * (EXP // 2), EXP // 2), EXP // 2)
    core_w = send(w_sum.at[there], w_core, rc_s.at[0], rc_r.at[0], sibling)
    core_o = send(o_sum.at[there], o_core, rc_s.at[1], rc_r.at[1], sibling)
    for d in (2, 6, 1, 7, 0):
        term(d)

    pass_on(0, 2)
    pass_on(1, 2)

    core_w.wait_recv()
    core_o.wait_recv()
    w_mid[...] = (w_sum[here, :] + w_core[...]).reshape(NX, 16, D)
    o_mid[...] = (o_sum[here, :].astype(F32) + o_core[...].astype(F32)).astype(BF16).reshape(NX, 16, D)
    mid_sums = []
    for j in range(1, NX):
        to = lax.rem(b + j, NX)
        device = {"seq": seq_of(a, to)}
        mid_sums.append(send(w_mid.at[to], w_min.at[j - 1], rm_s.at[0, j - 1], rm_r.at[0, j - 1], device))
        mid_sums.append(send(o_mid.at[to], o_min.at[j - 1], rm_s.at[1, j - 1], rm_r.at[1, j - 1], device))

    pass_on(0, 3)
    pass_on(1, 3)
    pass_on(0, 4)
    pass_on(1, 4)

    for copy in mid_sums:
        copy.wait_recv()
    w16 = w_mid[b]
    o16 = o_mid[b].astype(F32)
    for j in range(NX - 1):
        w16 = w16 + w_min[j]
        o16 = o16 + o_min[j].astype(F32)
    for j in range(NY):
        w_end[j] = w16[4 * j:4 * j + 4]
        o_end[j] = o16[4 * j:4 * j + 4]
    slot = dp * NY + a
    w_ein[slot] = w_end[a]
    end_w, end_o = [], []
    for j in range(NY):
        to = lax.rem(a + j, NY)
        device = seq_of(to, b)
        end_w.append(
            send(w_end.at[to], w_ein.at[slot], re_s.at[0, j], re_r.at[0, j], {"dp": 1 - dp, "seq": device})
        )
        if j > 0:
            end_w.append(send(w_end.at[to], w_ein.at[slot], re_s.at[1, j], re_r.at[1, j], {"seq": device}))
            end_o.append(send(o_end.at[to], o_ein.at[j - 1], re_s.at[2, j], re_r.at[2, j], {"seq": device}))

    pass_on(0, 5)
    pass_on(1, 5)

    for copy in end_o:
        copy.wait_recv()
    total = o_end[a]
    for j in range(NY - 1):
        total = total + o_ein[j]
    so_ref[...] = total.astype(BF16)

    pass_on(0, 6)
    pass_on(1, 6)

    for copy in end_w:
        copy.wait_recv()
    total = w_ein[0]
    for j in range(1, 2 * NY):
        total = total + w_ein[j]
    sw_ref[...] = total

    for h in (1, 0):
        value = part[0, HALF * h:HALF * (h + 1), :]
        for way in range(2):
            j, copy = ring[way][(1, h)]
            copy.wait_recv()
            value = value + ring_in[way, j].astype(F32)
        tg_ref[HALF * h:HALF * (h + 1), :] = value.astype(BF16)

    for copy in pending:
        copy.wait_send()
    pltpu.make_async_copy(row_all, row_all, stat_s.at[0]).wait()
    pltpu.make_async_copy(col_all, col_all, stat_s.at[1]).wait()


def write_out(*refs):
    sems = refs[-1]
    copies = [pltpu.make_async_copy(refs[i], refs[3 + i], sems.at[i]) for i in range(3)]
    for copy in copies:
        copy.start()
    for copy in copies:
        copy.wait()


def on_device(tokens, slot_weight, slot_output, slot_input_grad, output_grad):
    vmem = pl.BlockSpec(memory_space=pltpu.VMEM)
    hbm = pl.BlockSpec(memory_space=pl.ANY)
    dma = pltpu.SemaphoreType.DMA
    shapes = (
        jax.ShapeDtypeStruct((OWN, D), BF16),
        jax.ShapeDtypeStruct((4, D), BF16),
        jax.ShapeDtypeStruct((4, D), F32),
    )
    results = pl.pallas_call(
        kernel,
        out_shape=shapes,
        in_specs=[hbm, hbm, hbm, hbm, hbm],
        out_specs=(vmem, vmem, vmem),
        scratch_shapes=[
            pltpu.VMEM((TOK, D), BF16),
            pltpu.VMEM((TOK, D), BF16),
            pltpu.VMEM((NY, 3, 4, D), BF16),
            pltpu.VMEM((3, NC, NX, 16, D), BF16),
            pltpu.VMEM((EXP, TOK), F32),
            pltpu.VMEM((EXP, TOK), F32),
            pltpu.VMEM((EXP, TOK), F32),
            pltpu.VMEM((EXP, TOK), F32),
            pltpu.VMEM((EXP, TOK), F32),
            pltpu.VMEM((EXP, EXP), F32),
            pltpu.VMEM((NZ, 2, TOK), F32),
            pltpu.VMEM((NSEQ, 2, EXP), F32),
            pltpu.VMEM((3 * EXP, TOK), BF16),
            pltpu.VMEM((EXP, TOK), BF16),
            pltpu.VMEM((TOK, 2 * EXP), BF16),
            pltpu.VMEM((NZ, OWN, D), F32),
            pltpu.VMEM((2, 7, HALF, D), BF16),
            pltpu.VMEM((2, 7, HALF, D), BF16),
            pltpu.VMEM((EXP, D), F32),
            pltpu.VMEM((EXP, D), BF16),
            pltpu.VMEM((EXP // 2, D), F32),
            pltpu.VMEM((EXP // 2, D), BF16),
            pltpu.VMEM((NX, 16, D), F32),
            pltpu.VMEM((NX, 16, D), BF16),
            pltpu.VMEM((NX - 1, 16, D), F32),
            pltpu.VMEM((NX - 1, 16, D), BF16),
            pltpu.VMEM((NY, 4, D), F32),
            pltpu.VMEM((NY, 4, D), F32),
            pltpu.VMEM((2 * NY, 4, D), F32),
            pltpu.VMEM((NY - 1, 4, D), F32),
            dma((5,)),
            dma((3, 3)), dma((3, 3)),
            dma((3,)), dma((3,)),
            dma((4,)), dma((4,)),
            dma((2,)), dma((2,)),
            dma((2, 7)), dma((2, 7)),
            dma((2,)), dma((2,)),
            dma((2, 3)), dma((2, 3)),
            dma((3, 4)), dma((3, 4)),
        ],
        compiler_params=pltpu.CompilerParams(
            collective_id=0, has_side_effects=True, vmem_limit_bytes=60 * 1024 * 1024
        ),
        cost_estimate=pl.CostEstimate(
            flops=2_000_000_000, bytes_accessed=5_000_000, transcendentals=250_000
        ),
    )(tokens[0], slot_weight, slot_output[0], slot_input_grad[0], output_grad[0])
    token_grad, slot_output_grad, slot_weight_grad = pl.pallas_call(
        write_out,
        out_shape=shapes,
        in_specs=[hbm] * 3,
        out_specs=(hbm,) * 3,
        scratch_shapes=[dma((3,))],
    )(*results)
    return (token_grad[None], slot_output_grad[None], slot_weight_grad)


def solution(mesh):
    placed = (
        P("dp", "seq", None),
        P(("seq", "expert"), None),
        P("dp", ("seq", "expert"), None),
        P("dp", ("seq", "expert"), None),
        P("dp", "seq", None),
    )
    return jax.shard_map(
        on_device,
        mesh=mesh,
        in_specs=placed,
        out_specs=(
            P("dp", ("seq", "expert"), None),
            P("dp", ("seq", "expert"), None),
            P(("seq", "expert"), None),
        ),
        check_vma=False,
    )
```

```python
import jax
import jax.numpy as jnp
from jax import lax
from jax.experimental import pallas as pl
from jax.experimental.pallas import tpu as pltpu
from jax.sharding import PartitionSpec as P

F32 = jnp.float32
BF16 = jnp.bfloat16
MESH = pl.DeviceIdType.MESH

NY, NX, NC, NZ = 4, 4, 2, 8
NSEQ = NY * NX * NC
D = 1280
TOK = 768
EXP = 128
OWN = TOK // NZ
HALF = OWN // 2

RIGHT = ((4, 0), (3, 1), (3, 0), (2, 1), (2, 0), (1, 1), (1, 0))
LEFT = ((4, 1), (3, 0), (3, 1), (2, 0), (2, 1), (1, 0), (1, 1))


def nt_dot(a, b):
    return lax.dot_general(a, b, (((1,), (1,)), ((), ())), preferred_element_type=F32)


def nn_dot(a, b):
    return jnp.dot(a, b, preferred_element_type=F32)


def kernel(
    tok_hbm, own_ref, og_hbm,
    tg_ref, so_ref, sw_ref,
    tok, og, shard, shard_out, params, outs, logit, cgrad, dgrad, row_exp, col_exp, col_tile, row_stat, col_stat,
    mat, comb, fac, part, stage, ring_in,
    w_sum, o_sum, w_core, o_core, w_mid, o_mid, w_min, o_min, w_end, o_end, w_ein, o_ein,
    load_sem, ys, yr, xs, xr, cs, cr, stat_s, stat_r, ring_s, ring_r, rc_s, rc_r, rm_s, rm_r, re_s, re_r,
):
    dp = lax.axis_index("dp")
    seq = lax.axis_index("seq")
    z = lax.axis_index("expert")
    core = lax.rem(seq, NC)
    x = lax.rem(seq // NC, NX)
    y = seq // (NC * NX)

    def seq_of(yy, xx):
        return (yy * NX + xx) * NC + core

    barrier = pltpu.get_barrier_semaphore()

    def greet(device):
        pl.semaphore_signal(barrier, inc=1, device_id=device, device_id_type=MESH)

    @pl.loop(1, NSEQ)
    def _(j):
        greet({"seq": lax.rem(seq + j, NSEQ)})

    @pl.loop(1, NZ)
    def _(j):
        greet({"expert": lax.rem(z + j, NZ)})

    for j in range(NY):
        greet({"dp": 1 - dp, "seq": seq_of(lax.rem(y + j, NY), x)})

    load_tok = pltpu.make_async_copy(tok_hbm, tok, load_sem.at[0])
    load_og = pltpu.make_async_copy(og_hbm, og, load_sem.at[1])
    load_tok.start()
    load_og.start()
    pl.semaphore_wait(barrier, NSEQ + NZ - 2 + NY)

    pending = []

    def send(src, dst, s_sem, r_sem, device):
        copy = pltpu.make_async_remote_copy(
            src_ref=src, dst_ref=dst, send_sem=s_sem, recv_sem=r_sem,
            device_id=device, device_id_type=MESH,
        )
        copy.start()
        pending.append(copy)
        return copy

    pair_near, out_near, pair_far, out_far = [], [], [], []
    for j in range(1, NX):
        x_peer, y_peer = seq_of(y, lax.rem(x + j, NX)), seq_of(lax.rem(y + j, NY), x)
        out_near.append(
            send(own_ref.at[2], shard_out.at[x], xs.at[0, j - 1], xr.at[0, j - 1], {"seq": x_peer})
        )
        pair_near.append(
            send(own_ref.at[pl.ds(0, 2)], shard.at[y], ys.at[0, j - 1], yr.at[0, j - 1], {"seq": y_peer})
        )
    shard_out[x] = own_ref[2]
    shard[y] = own_ref[0:2]
    sibling = {"seq": seq + 1 - 2 * core}
    for copy in out_near:
        copy.wait_recv()
    rows = [shard_out[j].astype(F32) for j in range(NX)]
    outs[core, y] = jnp.concatenate(rows, axis=0).astype(BF16)
    own_out = outs.at[core, y]
    for j in range(1, NY):
        out_far.append(
            send(own_out, own_out, ys.at[1, j - 1], yr.at[1, j - 1], {"seq": seq_of(lax.rem(y + j, NY), x)})
        )
    for copy in pair_near:
        copy.wait_recv()
    for t in range(2):
        rows = [shard[j, t].astype(F32) for j in range(NY)]
        params[t, core, x] = jnp.concatenate(rows, axis=0).astype(BF16)
    own_pair = params.at[:, core, x]
    for j in range(1, NX):
        pair_far.append(
            send(own_pair, own_pair, xs.at[1, j - 1], xr.at[1, j - 1], {"seq": seq_of(y, lax.rem(x + j, NX))})
        )
    c_copies = [
        send(own_out, own_out, cs.at[1, 0], cr.at[1, 0], sibling),
        send(own_pair, own_pair, cs.at[0, 0], cr.at[0, 0], sibling),
    ]
    for j in (1, 3, 2):
        out_far[j - 1].wait_recv()
        block = outs.at[core, lax.rem(y - j + NY, NY)]
        c_copies.append(send(block, block, cs.at[1, j], cr.at[1, j], sibling))
        pair_far[j - 1].wait_recv()
        block = params.at[:, core, lax.rem(x - j + NX, NX)]
        c_copies.append(send(block, block, cs.at[0, j], cr.at[0, j], sibling))
    load_tok.wait()
    load_og.wait()
    for copy in c_copies:
        copy.wait_recv()

    both = params[...].reshape(2 * EXP, D)
    slot_outs = outs[...].reshape(EXP, D)
    for n in range(TOK // 256):
        cols = slice(256 * n, 256 * (n + 1))
        pair = nt_dot(both, tok[cols, :])
        logit[:, cols] = pair[:EXP]
        dgrad[:, cols] = pair[EXP:]
        swapped = nt_dot(slot_outs, og[cols, :])
        for c in range(NC):
            for yy in range(NY):
                for xx in range(NX):
                    put, get = (c * NX + xx) * 16 + 4 * yy, (c * NY + yy) * 16 + 4 * xx
                    cgrad[put:put + 4, cols] = swapped[get:get + 4]

    ROWS = 16
    blocks = [slice(ROWS * b, ROWS * (b + 1)) for b in range(EXP // ROWS)]
    top = logit[blocks[0], :]
    for rows in blocks[1:]:
        top = jnp.maximum(top, logit[rows, :])
    row_max = jnp.max(top, axis=0, keepdims=True)
    row_sum = jnp.zeros((ROWS, TOK), F32)
    row_dot = jnp.zeros((ROWS, TOK), F32)
    lane = lax.broadcasted_iota(jnp.int32, (ROWS, EXP), 1)
    for rows in blocks:
        value = logit[rows, :]
        by_row = jnp.exp(value - row_max)
        row_exp[rows, :] = by_row
        row_sum = row_sum + by_row
        row_dot = row_dot + by_row * cgrad[rows, :]
        col_max = jnp.max(value, axis=1, keepdims=True)
        by_col = jnp.exp(value - col_max)
        col_exp[rows, :] = by_col
        col_sum = jnp.sum(by_col, axis=1, keepdims=True)
        col_dot = jnp.sum(by_col * dgrad[rows, :], axis=1, keepdims=True)
        col_tile[rows, :] = jnp.where(
            lane == 0,
            col_max + jnp.log(col_sum),
            jnp.where(lane == 1, col_dot / col_sum, jnp.where(lane == 2, col_max, 0.0)),
        )
    row_sum = jnp.sum(row_sum, axis=0, keepdims=True)
    row_dot = jnp.sum(row_dot, axis=0, keepdims=True)
    row_stat[z] = jnp.concatenate([row_max + jnp.log(row_sum), row_dot / row_sum], axis=0)
    turned = col_tile[...].T
    col_stat[seq] = turned[0:2, :]
    col_top = turned[2:3, :]
    @pl.loop(1, NZ)
    def _(j):
        pltpu.make_async_remote_copy(
            src_ref=row_stat.at[z], dst_ref=row_stat.at[z],
            send_sem=stat_s.at[0], recv_sem=stat_r.at[0],
            device_id={"expert": lax.rem(z + j, NZ)}, device_id_type=MESH,
        ).start()

    @pl.loop(1, NSEQ)
    def _(j):
        pltpu.make_async_remote_copy(
            src_ref=col_stat.at[seq], dst_ref=col_stat.at[seq],
            send_sem=stat_s.at[1], recv_sem=stat_r.at[1],
            device_id={"seq": lax.rem(seq + j, NSEQ)}, device_id_type=MESH,
        ).start()

    row_all = row_stat.at[pl.ds(0, NZ - 1)]
    col_all = col_stat.at[pl.ds(0, NSEQ - 1)]
    pltpu.make_async_copy(row_all, row_all, stat_r.at[0]).wait()

    def join(stat, count):
        best = stat[0][0:1]
        for j in range(1, count):
            best = jnp.maximum(best, stat[j][0:1])
        mass = jnp.zeros_like(best)
        mean = jnp.zeros_like(best)
        for j in range(count):
            one = stat[j]
            weight = jnp.exp(one[0:1] - best)
            mass = mass + weight
            mean = mean + weight * one[1:2]
        return best, mass, mean / mass

    best, mass, row_mean = join(row_stat, NZ)
    row_scale = jnp.exp(row_max - best) / mass
    pltpu.make_async_copy(col_all, col_all, stat_r.at[1]).wait()
    best, mass, col_mean = join(col_stat, NSEQ)
    lines = lax.broadcasted_iota(jnp.int32, (EXP, EXP), 0)
    col_tile[...] = jnp.where(
        lines == 0, jnp.exp(col_top - best) / mass, jnp.where(lines == 1, col_mean, 0.0)
    ).T

    for n, rows in enumerate(blocks):
        combine = row_exp[rows, :] * row_scale
        dispatch = col_exp[rows, :] * col_tile[rows, 0:1]
        grad = combine * (cgrad[rows, :] - row_mean) + dispatch * (dgrad[rows, :] - col_tile[rows, 1:2])
        high = grad.astype(BF16)
        mat[rows, :] = (grad - high.astype(F32)).astype(BF16)
        mat[EXP + ROWS * n:EXP + ROWS * (n + 1), :] = high
        mat[2 * EXP + ROWS * n:2 * EXP + ROWS * (n + 1), :] = dispatch.astype(BF16)
        comb[rows, :] = combine.astype(BF16)
    fac[...] = mat[EXP:3 * EXP, :].T

    def term(d):
        stacked = params[...].reshape(2 * EXP, D)
        owner = lax.rem(z + d, NZ)
        part[d] = nn_dot(fac[pl.ds(pl.multiple_of(owner * OWN, OWN), OWN), :], stacked)

    ring = ({}, {})
    towards = ({"expert": lax.rem(z + 1, NZ)}, {"expert": lax.rem(z + NZ - 1, NZ)})

    def pass_on(way, i):
        d, h = (RIGHT, LEFT)[way][i]
        value = part[d if way == 0 else NZ - d, HALF * h:HALF * (h + 1), :]
        if (d + 1, h) in ring[way]:
            j, copy = ring[way][(d + 1, h)]
            copy.wait_recv()
            value = value + ring_in[way, j].astype(F32)
        stage[way, i] = value.astype(BF16)
        ring[way][(d, h)] = (
            i,
            send(stage.at[way, i], ring_in.at[way, i], ring_s.at[way, i], ring_r.at[way, i], towards[way]),
        )

    term(4)
    pass_on(0, 0)
    pass_on(1, 0)
    term(3)
    pass_on(0, 1)
    term(5)
    pass_on(1, 1)

    for n in range(D // 256):
        cols = slice(256 * n, 256 * (n + 1))
        pair = nn_dot(mat[0:2 * EXP, :], tok[:, cols])
        w_sum[:, cols] = pair[:EXP] + pair[EXP:]
        o_sum[:, cols] = nn_dot(comb[...], og[:, cols]).astype(BF16)
    there = pl.ds(pl.multiple_of((1 - core) * (EXP // 2), EXP // 2), EXP // 2)
    here = pl.ds(pl.multiple_of(core * (EXP // 2), EXP // 2), EXP // 2)
    core_w = send(w_sum.at[there], w_core, rc_s.at[0], rc_r.at[0], sibling)
    core_o = send(o_sum.at[there], o_core, rc_s.at[1], rc_r.at[1], sibling)
    for d in (2, 6, 1, 7, 0):
        term(d)

    pass_on(0, 2)
    pass_on(1, 2)

    core_w.wait_recv()
    core_o.wait_recv()
    w_mid[...] = (w_sum[here, :] + w_core[...]).reshape(NX, 16, D)
    o_mid[...] = (o_sum[here, :].astype(F32) + o_core[...].astype(F32)).astype(BF16).reshape(NX, 16, D)
    mid_sums = []
    for j in range(1, NX):
        to = lax.rem(x + j, NX)
        device = {"seq": seq_of(y, to)}
        mid_sums.append(send(w_mid.at[to], w_min.at[j - 1], rm_s.at[0, j - 1], rm_r.at[0, j - 1], device))
        mid_sums.append(send(o_mid.at[to], o_min.at[j - 1], rm_s.at[1, j - 1], rm_r.at[1, j - 1], device))

    pass_on(0, 3)
    pass_on(1, 3)
    pass_on(0, 4)
    pass_on(1, 4)

    for copy in mid_sums:
        copy.wait_recv()
    w16 = w_mid[x]
    o16 = o_mid[x].astype(F32)
    for j in range(NX - 1):
        w16 = w16 + w_min[j]
        o16 = o16 + o_min[j].astype(F32)
    for j in range(NY):
        w_end[j] = w16[4 * j:4 * j + 4]
        o_end[j] = o16[4 * j:4 * j + 4]
    slot = dp * NY + y
    w_ein[slot] = w_end[y]
    end_w, end_o = [], []
    for j in range(NY):
        to = lax.rem(y + j, NY)
        device = seq_of(to, x)
        end_w.append(
            send(w_end.at[to], w_ein.at[slot], re_s.at[0, j], re_r.at[0, j], {"dp": 1 - dp, "seq": device})
        )
        if j > 0:
            end_w.append(send(w_end.at[to], w_ein.at[slot], re_s.at[1, j], re_r.at[1, j], {"seq": device}))
            end_o.append(send(o_end.at[to], o_ein.at[j - 1], re_s.at[2, j], re_r.at[2, j], {"seq": device}))

    pass_on(0, 5)
    pass_on(1, 5)

    for copy in end_o:
        copy.wait_recv()
    total = o_end[y]
    for j in range(NY - 1):
        total = total + o_ein[j]
    so_ref[...] = total.astype(BF16)

    pass_on(0, 6)
    pass_on(1, 6)

    for copy in end_w:
        copy.wait_recv()
    total = w_ein[0]
    for j in range(1, 2 * NY):
        total = total + w_ein[j]
    sw_ref[...] = total

    for h in (1, 0):
        value = part[0, HALF * h:HALF * (h + 1), :]
        for way in range(2):
            j, copy = ring[way][(1, h)]
            copy.wait_recv()
            value = value + ring_in[way, j].astype(F32)
        tg_ref[HALF * h:HALF * (h + 1), :] = value.astype(BF16)

    for copy in pending:
        copy.wait_send()
    pltpu.make_async_copy(row_all, row_all, stat_s.at[0]).wait()
    pltpu.make_async_copy(col_all, col_all, stat_s.at[1]).wait()


def write_out(*refs):
    sems = refs[-1]
    copies = [pltpu.make_async_copy(refs[i], refs[3 + i], sems.at[i]) for i in range(3)]
    for copy in copies:
        copy.start()
    for copy in copies:
        copy.wait()


def on_device(tokens, slot_weight, slot_output, slot_input_grad, output_grad):
    vmem = pl.BlockSpec(memory_space=pltpu.VMEM)
    hbm = pl.BlockSpec(memory_space=pl.ANY)
    dma = pltpu.SemaphoreType.DMA
    shapes = (
        jax.ShapeDtypeStruct((OWN, D), BF16),
        jax.ShapeDtypeStruct((4, D), BF16),
        jax.ShapeDtypeStruct((4, D), F32),
    )
    own = jnp.concatenate([slot_weight[None], slot_input_grad, slot_output])
    results = pl.pallas_call(
        kernel,
        out_shape=shapes,
        in_specs=[hbm, vmem, hbm],
        out_specs=(vmem, vmem, vmem),
        scratch_shapes=[
            pltpu.VMEM((TOK, D), BF16),
            pltpu.VMEM((TOK, D), BF16),
            pltpu.VMEM((NY, 2, 4, D), BF16),
            pltpu.VMEM((NX, 4, D), BF16),
            pltpu.VMEM((2, NC, NX, 16, D), BF16),
            pltpu.VMEM((NC, NY, 16, D), BF16),
            pltpu.VMEM((EXP, TOK), F32),
            pltpu.VMEM((EXP, TOK), F32),
            pltpu.VMEM((EXP, TOK), F32),
            pltpu.VMEM((EXP, TOK), F32),
            pltpu.VMEM((EXP, TOK), F32),
            pltpu.VMEM((EXP, EXP), F32),
            pltpu.VMEM((NZ, 2, TOK), F32),
            pltpu.VMEM((NSEQ, 2, EXP), F32),
            pltpu.VMEM((3 * EXP, TOK), BF16),
            pltpu.VMEM((EXP, TOK), BF16),
            pltpu.VMEM((TOK, 2 * EXP), BF16),
            pltpu.VMEM((NZ, OWN, D), F32),
            pltpu.VMEM((2, 7, HALF, D), BF16),
            pltpu.VMEM((2, 7, HALF, D), BF16),
            pltpu.VMEM((EXP, D), F32),
            pltpu.VMEM((EXP, D), BF16),
            pltpu.VMEM((EXP // 2, D), F32),
            pltpu.VMEM((EXP // 2, D), BF16),
            pltpu.VMEM((NX, 16, D), F32),
            pltpu.VMEM((NX, 16, D), BF16),
            pltpu.VMEM((NX - 1, 16, D), F32),
            pltpu.VMEM((NX - 1, 16, D), BF16),
            pltpu.VMEM((NY, 4, D), F32),
            pltpu.VMEM((NY, 4, D), F32),
            pltpu.VMEM((2 * NY, 4, D), F32),
            pltpu.VMEM((NY - 1, 4, D), F32),
            dma((2,)),
            dma((2, 3)), dma((2, 3)),
            dma((2, 3)), dma((2, 3)),
            dma((2, 4)), dma((2, 4)),
            dma((2,)), dma((2,)),
            dma((2, 7)), dma((2, 7)),
            dma((2,)), dma((2,)),
            dma((2, 3)), dma((2, 3)),
            dma((3, 4)), dma((3, 4)),
        ],
        compiler_params=pltpu.CompilerParams(
            collective_id=0, has_side_effects=True, vmem_limit_bytes=62 * 1024 * 1024 + 512 * 1024
        ),
        cost_estimate=pl.CostEstimate(
            flops=2_000_000_000, bytes_accessed=5_000_000, transcendentals=250_000
        ),
    )(tokens[0], own, output_grad[0])
    token_grad, slot_output_grad, slot_weight_grad = pl.pallas_call(
        write_out,
        out_shape=shapes,
        in_specs=[vmem] * 3,
        out_specs=(hbm,) * 3,
        scratch_shapes=[dma((3,))],
    )(*results)
    return (token_grad[None], slot_output_grad[None], slot_weight_grad)


def solution(mesh):
    placed = (
        P("dp", "seq", None),
        P(("seq", "expert"), None),
        P("dp", ("seq", "expert"), None),
        P("dp", ("seq", "expert"), None),
        P("dp", "seq", None),
    )
    return jax.shard_map(
        on_device,
        mesh=mesh,
        in_specs=placed,
        out_specs=(
            P("dp", ("seq", "expert"), None),
            P("dp", ("seq", "expert"), None),
            P(("seq", "expert"), None),
        ),
        check_vma=False,
    )
```

```python
import jax
import jax.numpy as jnp
from jax import lax
from jax.experimental import pallas as pl
from jax.experimental.pallas import tpu as pltpu
from jax.sharding import PartitionSpec as P

F32 = jnp.float32
BF16 = jnp.bfloat16
MESH = pl.DeviceIdType.MESH

NY, NX, NC, NZ = 4, 4, 2, 8
NSEQ = NY * NX * NC
D = 1280
TOK = 768
EXP = 128
OWN = TOK // NZ
HALF = OWN // 2

RIGHT = ((4, 0), (3, 1), (3, 0), (2, 1), (2, 0), (1, 1), (1, 0))
LEFT = ((4, 1), (3, 0), (3, 1), (2, 0), (2, 1), (1, 0), (1, 1))


def nt_dot(a, b):
    return lax.dot_general(a, b, (((1,), (1,)), ((), ())), preferred_element_type=F32)


def nn_dot(a, b):
    return jnp.dot(a, b, preferred_element_type=F32)


def kernel(
    tok_hbm, phi_hbm, out_hbm, inp_hbm, og_hbm,
    tg_ref, so_ref, sw_ref,
    tok, og, own, shard, shard_out, params, outs, logit, cgrad, dgrad, row_exp, col_exp, col_tile, row_stat, col_stat,
    mat, comb, fac, part, stage, ring_in,
    w_sum, o_sum, w_core, o_core, w_mid, o_mid, w_min, o_min, w_end, o_end, w_ein, o_ein,
    load_sem, ys, yr, xs, xr, cs, cr, stat_s, stat_r, ring_s, ring_r, rc_s, rc_r, rm_s, rm_r, re_s, re_r,
):
    dp = lax.axis_index("dp")
    seq = lax.axis_index("seq")
    z = lax.axis_index("expert")
    core = lax.rem(seq, NC)
    x = lax.rem(seq // NC, NX)
    y = seq // (NC * NX)

    def seq_of(yy, xx):
        return (yy * NX + xx) * NC + core

    load_own = [
        pltpu.make_async_copy(src, own.at[t], load_sem.at[2 + t])
        for t, src in enumerate((phi_hbm, inp_hbm, out_hbm))
    ]
    for copy in load_own:
        copy.start()
    barrier = pltpu.get_barrier_semaphore()

    def greet(device):
        pl.semaphore_signal(barrier, inc=1, device_id=device, device_id_type=MESH)

    @pl.loop(1, NSEQ)
    def _(j):
        greet({"seq": lax.rem(seq + j, NSEQ)})

    @pl.loop(1, NZ)
    def _(j):
        greet({"expert": lax.rem(z + j, NZ)})

    for j in range(NY):
        greet({"dp": 1 - dp, "seq": seq_of(lax.rem(y + j, NY), x)})

    load_tok = pltpu.make_async_copy(tok_hbm, tok, load_sem.at[0])
    load_og = pltpu.make_async_copy(og_hbm, og, load_sem.at[1])
    load_tok.start()
    load_og.start()
    for copy in load_own:
        copy.wait()
    pl.semaphore_wait(barrier, NSEQ + NZ - 2 + NY)

    pending = []

    def send(src, dst, s_sem, r_sem, device):
        copy = pltpu.make_async_remote_copy(
            src_ref=src, dst_ref=dst, send_sem=s_sem, recv_sem=r_sem,
            device_id=device, device_id_type=MESH,
        )
        copy.start()
        pending.append(copy)
        return copy

    pair_near, out_near, pair_far, out_far = [], [], [], []
    for j in range(1, NX):
        x_peer, y_peer = seq_of(y, lax.rem(x + j, NX)), seq_of(lax.rem(y + j, NY), x)
        out_near.append(
            send(own.at[2], shard_out.at[x], xs.at[0, j - 1], xr.at[0, j - 1], {"seq": x_peer})
        )
        pair_near.append(
            send(own.at[pl.ds(0, 2)], shard.at[y], ys.at[0, j - 1], yr.at[0, j - 1], {"seq": y_peer})
        )
    shard_out[x] = own[2]
    shard[y] = own[0:2]
    sibling = {"seq": seq + 1 - 2 * core}
    for copy in out_near:
        copy.wait_recv()
    rows = [shard_out[j].astype(F32) for j in range(NX)]
    outs[core, y] = jnp.concatenate(rows, axis=0).astype(BF16)
    own_out = outs.at[core, y]
    for j in range(1, NY):
        out_far.append(
            send(own_out, own_out, ys.at[1, j - 1], yr.at[1, j - 1], {"seq": seq_of(lax.rem(y + j, NY), x)})
        )
    for copy in pair_near:
        copy.wait_recv()
    for t in range(2):
        rows = [shard[j, t].astype(F32) for j in range(NY)]
        params[t, core, x] = jnp.concatenate(rows, axis=0).astype(BF16)
    own_pair = params.at[:, core, x]
    for j in range(1, NX):
        pair_far.append(
            send(own_pair, own_pair, xs.at[1, j - 1], xr.at[1, j - 1], {"seq": seq_of(y, lax.rem(x + j, NX))})
        )
    c_copies = [
        send(own_out, own_out, cs.at[1, 0], cr.at[1, 0], sibling),
        send(own_pair, own_pair, cs.at[0, 0], cr.at[0, 0], sibling),
    ]
    for j in (1, 3, 2):
        out_far[j - 1].wait_recv()
        block = outs.at[core, lax.rem(y - j + NY, NY)]
        c_copies.append(send(block, block, cs.at[1, j], cr.at[1, j], sibling))
        pair_far[j - 1].wait_recv()
        block = params.at[:, core, lax.rem(x - j + NX, NX)]
        c_copies.append(send(block, block, cs.at[0, j], cr.at[0, j], sibling))
    load_tok.wait()
    load_og.wait()
    for copy in c_copies:
        copy.wait_recv()

    both = params[...].reshape(2 * EXP, D)
    slot_outs = outs[...].reshape(EXP, D)
    for n in range(TOK // 256):
        cols = slice(256 * n, 256 * (n + 1))
        pair = nt_dot(both, tok[cols, :])
        logit[:, cols] = pair[:EXP]
        dgrad[:, cols] = pair[EXP:]
        swapped = nt_dot(slot_outs, og[cols, :])
        for c in range(NC):
            for yy in range(NY):
                for xx in range(NX):
                    put, get = (c * NX + xx) * 16 + 4 * yy, (c * NY + yy) * 16 + 4 * xx
                    cgrad[put:put + 4, cols] = swapped[get:get + 4]

    ROWS = 16
    blocks = [slice(ROWS * b, ROWS * (b + 1)) for b in range(EXP // ROWS)]
    top = logit[blocks[0], :]
    for rows in blocks[1:]:
        top = jnp.maximum(top, logit[rows, :])
    row_max = jnp.max(top, axis=0, keepdims=True)
    row_sum = jnp.zeros((ROWS, TOK), F32)
    row_dot = jnp.zeros((ROWS, TOK), F32)
    lane = lax.broadcasted_iota(jnp.int32, (ROWS, EXP), 1)
    for rows in blocks:
        value = logit[rows, :]
        by_row = jnp.exp(value - row_max)
        row_exp[rows, :] = by_row
        row_sum = row_sum + by_row
        row_dot = row_dot + by_row * cgrad[rows, :]
        col_max = jnp.max(value, axis=1, keepdims=True)
        by_col = jnp.exp(value - col_max)
        col_exp[rows, :] = by_col
        col_sum = jnp.sum(by_col, axis=1, keepdims=True)
        col_dot = jnp.sum(by_col * dgrad[rows, :], axis=1, keepdims=True)
        col_tile[rows, :] = jnp.where(
            lane == 0,
            col_max + jnp.log(col_sum),
            jnp.where(lane == 1, col_dot / col_sum, jnp.where(lane == 2, col_max, 0.0)),
        )
    row_sum = jnp.sum(row_sum, axis=0, keepdims=True)
    row_dot = jnp.sum(row_dot, axis=0, keepdims=True)
    row_stat[z] = jnp.concatenate([row_max + jnp.log(row_sum), row_dot / row_sum], axis=0)
    turned = col_tile[...].T
    col_stat[seq] = turned[0:2, :]
    col_top = turned[2:3, :]
    @pl.loop(1, NZ)
    def _(j):
        pltpu.make_async_remote_copy(
            src_ref=row_stat.at[z], dst_ref=row_stat.at[z],
            send_sem=stat_s.at[0], recv_sem=stat_r.at[0],
            device_id={"expert": lax.rem(z + j, NZ)}, device_id_type=MESH,
        ).start()

    @pl.loop(1, NSEQ)
    def _(j):
        pltpu.make_async_remote_copy(
            src_ref=col_stat.at[seq], dst_ref=col_stat.at[seq],
            send_sem=stat_s.at[1], recv_sem=stat_r.at[1],
            device_id={"seq": lax.rem(seq + j, NSEQ)}, device_id_type=MESH,
        ).start()

    row_all = row_stat.at[pl.ds(0, NZ - 1)]
    col_all = col_stat.at[pl.ds(0, NSEQ - 1)]
    pltpu.make_async_copy(row_all, row_all, stat_r.at[0]).wait()

    def join(stat, count):
        best = stat[0][0:1]
        for j in range(1, count):
            best = jnp.maximum(best, stat[j][0:1])
        mass = jnp.zeros_like(best)
        mean = jnp.zeros_like(best)
        for j in range(count):
            one = stat[j]
            weight = jnp.exp(one[0:1] - best)
            mass = mass + weight
            mean = mean + weight * one[1:2]
        return best, mass, mean / mass

    best, mass, row_mean = join(row_stat, NZ)
    row_scale = jnp.exp(row_max - best) / mass
    pltpu.make_async_copy(col_all, col_all, stat_r.at[1]).wait()
    best, mass, col_mean = join(col_stat, NSEQ)
    lines = lax.broadcasted_iota(jnp.int32, (EXP, EXP), 0)
    col_tile[...] = jnp.where(
        lines == 0, jnp.exp(col_top - best) / mass, jnp.where(lines == 1, col_mean, 0.0)
    ).T

    for n, rows in enumerate(blocks):
        combine = row_exp[rows, :] * row_scale
        dispatch = col_exp[rows, :] * col_tile[rows, 0:1]
        grad = combine * (cgrad[rows, :] - row_mean) + dispatch * (dgrad[rows, :] - col_tile[rows, 1:2])
        high = grad.astype(BF16)
        mat[rows, :] = (grad - high.astype(F32)).astype(BF16)
        mat[EXP + ROWS * n:EXP + ROWS * (n + 1), :] = high
        mat[2 * EXP + ROWS * n:2 * EXP + ROWS * (n + 1), :] = dispatch.astype(BF16)
        comb[rows, :] = combine.astype(BF16)
    fac[...] = mat[EXP:3 * EXP, :].T

    def term(d):
        stacked = params[...].reshape(2 * EXP, D)
        owner = lax.rem(z + d, NZ)
        part[d] = nn_dot(fac[pl.ds(pl.multiple_of(owner * OWN, OWN), OWN), :], stacked)

    ring = ({}, {})
    towards = ({"expert": lax.rem(z + 1, NZ)}, {"expert": lax.rem(z + NZ - 1, NZ)})

    def pass_on(way, i):
        d, h = (RIGHT, LEFT)[way][i]
        value = part[d if way == 0 else NZ - d, HALF * h:HALF * (h + 1), :]
        if (d + 1, h) in ring[way]:
            j, copy = ring[way][(d + 1, h)]
            copy.wait_recv()
            value = value + ring_in[way, j].astype(F32)
        stage[way, i] = value.astype(BF16)
        ring[way][(d, h)] = (
            i,
            send(stage.at[way, i], ring_in.at[way, i], ring_s.at[way, i], ring_r.at[way, i], towards[way]),
        )

    term(4)
    pass_on(0, 0)
    pass_on(1, 0)
    term(3)
    pass_on(0, 1)
    term(5)
    pass_on(1, 1)

    for n in range(D // 256):
        cols = slice(256 * n, 256 * (n + 1))
        pair = nn_dot(mat[0:2 * EXP, :], tok[:, cols])
        w_sum[:, cols] = pair[:EXP] + pair[EXP:]
        o_sum[:, cols] = nn_dot(comb[...], og[:, cols]).astype(BF16)
    there = pl.ds(pl.multiple_of((1 - core) * (EXP // 2), EXP // 2), EXP // 2)
    here = pl.ds(pl.multiple_of(core * (EXP // 2), EXP // 2), EXP // 2)
    core_w = send(w_sum.at[there], w_core, rc_s.at[0], rc_r.at[0], sibling)
    core_o = send(o_sum.at[there], o_core, rc_s.at[1], rc_r.at[1], sibling)
    for d in (2, 6, 1, 7, 0):
        term(d)

    pass_on(0, 2)
    pass_on(1, 2)

    core_w.wait_recv()
    core_o.wait_recv()
    w_mid[...] = (w_sum[here, :] + w_core[...]).reshape(NX, 16, D)
    o_mid[...] = (o_sum[here, :].astype(F32) + o_core[...].astype(F32)).astype(BF16).reshape(NX, 16, D)
    mid_sums = []
    for j in range(1, NX):
        to = lax.rem(x + j, NX)
        device = {"seq": seq_of(y, to)}
        mid_sums.append(send(w_mid.at[to], w_min.at[j - 1], rm_s.at[0, j - 1], rm_r.at[0, j - 1], device))
        mid_sums.append(send(o_mid.at[to], o_min.at[j - 1], rm_s.at[1, j - 1], rm_r.at[1, j - 1], device))

    pass_on(0, 3)
    pass_on(1, 3)
    pass_on(0, 4)
    pass_on(1, 4)

    for copy in mid_sums:
        copy.wait_recv()
    w16 = w_mid[x]
    o16 = o_mid[x].astype(F32)
    for j in range(NX - 1):
        w16 = w16 + w_min[j]
        o16 = o16 + o_min[j].astype(F32)
    for j in range(NY):
        w_end[j] = w16[4 * j:4 * j + 4]
        o_end[j] = o16[4 * j:4 * j + 4]
    slot = dp * NY + y
    w_ein[slot] = w_end[y]
    end_w, end_o = [], []
    for j in range(NY):
        to = lax.rem(y + j, NY)
        device = seq_of(to, x)
        end_w.append(
            send(w_end.at[to], w_ein.at[slot], re_s.at[0, j], re_r.at[0, j], {"dp": 1 - dp, "seq": device})
        )
        if j > 0:
            end_w.append(send(w_end.at[to], w_ein.at[slot], re_s.at[1, j], re_r.at[1, j], {"seq": device}))
            end_o.append(send(o_end.at[to], o_ein.at[j - 1], re_s.at[2, j], re_r.at[2, j], {"seq": device}))

    pass_on(0, 5)
    pass_on(1, 5)

    for copy in end_o:
        copy.wait_recv()
    total = o_end[y]
    for j in range(NY - 1):
        total = total + o_ein[j]
    so_ref[...] = total.astype(BF16)

    pass_on(0, 6)
    pass_on(1, 6)

    for copy in end_w:
        copy.wait_recv()
    total = w_ein[0]
    for j in range(1, 2 * NY):
        total = total + w_ein[j]
    sw_ref[...] = total

    for h in (1, 0):
        value = part[0, HALF * h:HALF * (h + 1), :]
        for way in range(2):
            j, copy = ring[way][(1, h)]
            copy.wait_recv()
            value = value + ring_in[way, j].astype(F32)
        tg_ref[HALF * h:HALF * (h + 1), :] = value.astype(BF16)

    for copy in pending:
        copy.wait_send()
    pltpu.make_async_copy(row_all, row_all, stat_s.at[0]).wait()
    pltpu.make_async_copy(col_all, col_all, stat_s.at[1]).wait()


def write_out(*refs):
    sems = refs[-1]
    copies = [pltpu.make_async_copy(refs[i], refs[3 + i], sems.at[i]) for i in range(3)]
    for copy in copies:
        copy.start()
    for copy in copies:
        copy.wait()


def on_device(tokens, slot_weight, slot_output, slot_input_grad, output_grad):
    vmem = pl.BlockSpec(memory_space=pltpu.VMEM)
    hbm = pl.BlockSpec(memory_space=pl.ANY)
    dma = pltpu.SemaphoreType.DMA
    shapes = (
        jax.ShapeDtypeStruct((OWN, D), BF16),
        jax.ShapeDtypeStruct((4, D), BF16),
        jax.ShapeDtypeStruct((4, D), F32),
    )
    results = pl.pallas_call(
        kernel,
        out_shape=shapes,
        in_specs=[hbm] * 5,
        out_specs=(vmem, vmem, vmem),
        scratch_shapes=[
            pltpu.VMEM((TOK, D), BF16),
            pltpu.VMEM((TOK, D), BF16),
            pltpu.VMEM((3, 4, D), BF16),
            pltpu.VMEM((NY, 2, 4, D), BF16),
            pltpu.VMEM((NX, 4, D), BF16),
            pltpu.VMEM((2, NC, NX, 16, D), BF16),
            pltpu.VMEM((NC, NY, 16, D), BF16),
            pltpu.VMEM((EXP, TOK), F32),
            pltpu.VMEM((EXP, TOK), F32),
            pltpu.VMEM((EXP, TOK), F32),
            pltpu.VMEM((EXP, TOK), F32),
            pltpu.VMEM((EXP, TOK), F32),
            pltpu.VMEM((EXP, EXP), F32),
            pltpu.VMEM((NZ, 2, TOK), F32),
            pltpu.VMEM((NSEQ, 2, EXP), F32),
            pltpu.VMEM((3 * EXP, TOK), BF16),
            pltpu.VMEM((EXP, TOK), BF16),
            pltpu.VMEM((TOK, 2 * EXP), BF16),
            pltpu.VMEM((NZ, OWN, D), F32),
            pltpu.VMEM((2, 7, HALF, D), BF16),
            pltpu.VMEM((2, 7, HALF, D), BF16),
            pltpu.VMEM((EXP, D), F32),
            pltpu.VMEM((EXP, D), BF16),
            pltpu.VMEM((EXP // 2, D), F32),
            pltpu.VMEM((EXP // 2, D), BF16),
            pltpu.VMEM((NX, 16, D), F32),
            pltpu.VMEM((NX, 16, D), BF16),
            pltpu.VMEM((NX - 1, 16, D), F32),
            pltpu.VMEM((NX - 1, 16, D), BF16),
            pltpu.VMEM((NY, 4, D), F32),
            pltpu.VMEM((NY, 4, D), F32),
            pltpu.VMEM((2 * NY, 4, D), F32),
            pltpu.VMEM((NY - 1, 4, D), F32),
            dma((5,)),
            dma((2, 3)), dma((2, 3)),
            dma((2, 3)), dma((2, 3)),
            dma((2, 4)), dma((2, 4)),
            dma((2,)), dma((2,)),
            dma((2, 7)), dma((2, 7)),
            dma((2,)), dma((2,)),
            dma((2, 3)), dma((2, 3)),
            dma((3, 4)), dma((3, 4)),
        ],
        compiler_params=pltpu.CompilerParams(
            collective_id=0, has_side_effects=True, vmem_limit_bytes=62 * 1024 * 1024 + 512 * 1024
        ),
        cost_estimate=pl.CostEstimate(
            flops=2_000_000_000, bytes_accessed=5_000_000, transcendentals=250_000
        ),
    )(tokens[0], slot_weight, slot_output[0], slot_input_grad[0], output_grad[0])
    token_grad, slot_output_grad, slot_weight_grad = pl.pallas_call(
        write_out,
        out_shape=shapes,
        in_specs=[vmem] * 3,
        out_specs=(hbm,) * 3,
        scratch_shapes=[dma((3,))],
    )(*results)
    return (token_grad[None], slot_output_grad[None], slot_weight_grad)


def solution(mesh):
    placed = (
        P("dp", "seq", None),
        P(("seq", "expert"), None),
        P("dp", ("seq", "expert"), None),
        P("dp", ("seq", "expert"), None),
        P("dp", "seq", None),
    )
    return jax.shard_map(
        on_device,
        mesh=mesh,
        in_specs=placed,
        out_specs=(
            P("dp", ("seq", "expert"), None),
            P("dp", ("seq", "expert"), None),
            P(("seq", "expert"), None),
        ),
        check_vma=False,
    )
```

```python
import jax
import jax.numpy as jnp
from jax import lax
from jax.experimental import pallas as pl
from jax.experimental.pallas import tpu as pltpu
from jax.sharding import PartitionSpec as P

F32 = jnp.float32
BF16 = jnp.bfloat16
MESH = pl.DeviceIdType.MESH

NY, NX, NC, NZ = 4, 4, 2, 8
CHIPS = NY * NX
D = 1280
TOK = 768
EXP = 128
OWN = TOK // NZ
HALF = OWN // 2

RIGHT = ((4, 0), (3, 1), (3, 0), (2, 1), (2, 0), (1, 1), (1, 0))
LEFT = ((4, 1), (3, 0), (3, 1), (2, 0), (2, 1), (1, 0), (1, 1))


def nt_dot(a, b):
    return lax.dot_general(a, b, (((1,), (1,)), ((), ())), preferred_element_type=F32)


def nn_dot(a, b):
    return jnp.dot(a, b, preferred_element_type=F32)


def kernel(
    tok_hbm, phi_hbm, out_hbm, inp_hbm, og_hbm,
    tg_ref, so_ref, sw_ref,
    tok, og, own, shard, shard_out, params, outs, logit, cgrad, dgrad, row_exp, col_exp, col_tile, row_stat, col_stat, col_pair,
    mat, comb, fac, part, stage, ring_in,
    w_sum, o_sum, w_core, o_core, w_mid, o_mid, w_min, o_min, w_end, o_end, w_ein, o_ein,
    load_sem, ys, yr, xs, xr, cs, cr, stat_s, stat_r, pair_s, pair_r, ring_s, ring_r, rc_s, rc_r, rm_s, rm_r, re_s, re_r,
):
    dp = lax.axis_index("dp")
    seq = lax.axis_index("seq")
    z = lax.axis_index("expert")
    core = lax.rem(seq, NC)
    x = lax.rem(seq // NC, NX)
    y = seq // (NC * NX)

    def seq_of(yy, xx):
        return (yy * NX + xx) * NC + core

    load_own = [
        pltpu.make_async_copy(src, own.at[t], load_sem.at[2 + t])
        for t, src in enumerate((phi_hbm, inp_hbm, out_hbm))
    ]
    for copy in load_own:
        copy.start()
    barrier = pltpu.get_barrier_semaphore()

    def greet(device):
        pl.semaphore_signal(barrier, inc=1, device_id=device, device_id_type=MESH)

    chip = y * NX + x
    sibling = {"seq": seq + 1 - 2 * core}
    greet(sibling)

    @pl.loop(1, CHIPS)
    def _(j):
        greet({"seq": lax.rem(chip + j, CHIPS) * NC + core})

    @pl.loop(1, NZ)
    def _(j):
        greet({"expert": lax.rem(z + j, NZ)})

    for j in range(NY):
        greet({"dp": 1 - dp, "seq": seq_of(lax.rem(y + j, NY), x)})

    load_tok = pltpu.make_async_copy(tok_hbm, tok, load_sem.at[0])
    load_og = pltpu.make_async_copy(og_hbm, og, load_sem.at[1])
    load_tok.start()
    load_og.start()
    for copy in load_own:
        copy.wait()
    pl.semaphore_wait(barrier, CHIPS + NZ - 1 + NY)

    pending = []

    def send(src, dst, s_sem, r_sem, device):
        copy = pltpu.make_async_remote_copy(
            src_ref=src, dst_ref=dst, send_sem=s_sem, recv_sem=r_sem,
            device_id=device, device_id_type=MESH,
        )
        copy.start()
        pending.append(copy)
        return copy

    pair_near, out_near, pair_far, out_far = [], [], [], []
    for j in range(1, NX):
        x_peer, y_peer = seq_of(y, lax.rem(x + j, NX)), seq_of(lax.rem(y + j, NY), x)
        out_near.append(
            send(own.at[2], shard_out.at[x], xs.at[0, j - 1], xr.at[0, j - 1], {"seq": x_peer})
        )
        pair_near.append(
            send(own.at[pl.ds(0, 2)], shard.at[y], ys.at[0, j - 1], yr.at[0, j - 1], {"seq": y_peer})
        )
    shard_out[x] = own[2]
    shard[y] = own[0:2]
    for copy in out_near:
        copy.wait_recv()
    rows = [shard_out[j].astype(F32) for j in range(NX)]
    outs[core, y] = jnp.concatenate(rows, axis=0).astype(BF16)
    own_out = outs.at[core, y]
    for j in range(1, NY):
        out_far.append(
            send(own_out, own_out, ys.at[1, j - 1], yr.at[1, j - 1], {"seq": seq_of(lax.rem(y + j, NY), x)})
        )
    for copy in pair_near:
        copy.wait_recv()
    for t in range(2):
        rows = [shard[j, t].astype(F32) for j in range(NY)]
        params[t, core, x] = jnp.concatenate(rows, axis=0).astype(BF16)
    own_pair = params.at[:, core, x]
    for j in range(1, NX):
        pair_far.append(
            send(own_pair, own_pair, xs.at[1, j - 1], xr.at[1, j - 1], {"seq": seq_of(y, lax.rem(x + j, NX))})
        )
    c_copies = [
        send(own_out, own_out, cs.at[1, 0], cr.at[1, 0], sibling),
        send(own_pair, own_pair, cs.at[0, 0], cr.at[0, 0], sibling),
    ]
    for j in (1, 3, 2):
        out_far[j - 1].wait_recv()
        block = outs.at[core, lax.rem(y - j + NY, NY)]
        c_copies.append(send(block, block, cs.at[1, j], cr.at[1, j], sibling))
        pair_far[j - 1].wait_recv()
        block = params.at[:, core, lax.rem(x - j + NX, NX)]
        c_copies.append(send(block, block, cs.at[0, j], cr.at[0, j], sibling))
    load_tok.wait()
    load_og.wait()
    for copy in c_copies:
        copy.wait_recv()

    both = params[...].reshape(2 * EXP, D)
    slot_outs = outs[...].reshape(EXP, D)
    for n in range(TOK // 256):
        cols = slice(256 * n, 256 * (n + 1))
        pair = nt_dot(both, tok[cols, :])
        logit[:, cols] = pair[:EXP]
        dgrad[:, cols] = pair[EXP:]
        swapped = nt_dot(slot_outs, og[cols, :])
        for c in range(NC):
            for yy in range(NY):
                for xx in range(NX):
                    put, get = (c * NX + xx) * 16 + 4 * yy, (c * NY + yy) * 16 + 4 * xx
                    cgrad[put:put + 4, cols] = swapped[get:get + 4]

    ROWS = 16
    blocks = [slice(ROWS * b, ROWS * (b + 1)) for b in range(EXP // ROWS)]
    top = logit[blocks[0], :]
    for rows in blocks[1:]:
        top = jnp.maximum(top, logit[rows, :])
    row_max = jnp.max(top, axis=0, keepdims=True)
    row_sum = jnp.zeros((ROWS, TOK), F32)
    row_dot = jnp.zeros((ROWS, TOK), F32)
    lane = lax.broadcasted_iota(jnp.int32, (ROWS, EXP), 1)
    for rows in blocks:
        value = logit[rows, :]
        by_row = jnp.exp(value - row_max)
        row_exp[rows, :] = by_row
        row_sum = row_sum + by_row
        row_dot = row_dot + by_row * cgrad[rows, :]
        col_max = jnp.max(value, axis=1, keepdims=True)
        by_col = jnp.exp(value - col_max)
        col_exp[rows, :] = by_col
        col_sum = jnp.sum(by_col, axis=1, keepdims=True)
        col_dot = jnp.sum(by_col * dgrad[rows, :], axis=1, keepdims=True)
        col_tile[rows, :] = jnp.where(
            lane == 0,
            col_max + jnp.log(col_sum),
            jnp.where(lane == 1, col_dot / col_sum, jnp.where(lane == 2, col_max, 0.0)),
        )
    row_sum = jnp.sum(row_sum, axis=0, keepdims=True)
    row_dot = jnp.sum(row_dot, axis=0, keepdims=True)
    row_stat[z] = jnp.concatenate([row_max + jnp.log(row_sum), row_dot / row_sum], axis=0)
    turned = col_tile[...].T
    col_pair[core] = turned[0:2, :]
    col_top = turned[2:3, :]
    pair_copy = send(col_pair.at[core], col_pair.at[core], pair_s, pair_r, sibling)

    @pl.loop(1, NZ)
    def _(j):
        pltpu.make_async_remote_copy(
            src_ref=row_stat.at[z], dst_ref=row_stat.at[z],
            send_sem=stat_s.at[0], recv_sem=stat_r.at[0],
            device_id={"expert": lax.rem(z + j, NZ)}, device_id_type=MESH,
        ).start()

    def join(stat, count):
        best = stat[0][0:1]
        for j in range(1, count):
            best = jnp.maximum(best, stat[j][0:1])
        mass = jnp.zeros_like(best)
        mean = jnp.zeros_like(best)
        for j in range(count):
            one = stat[j]
            weight = jnp.exp(one[0:1] - best)
            mass = mass + weight
            mean = mean + weight * one[1:2]
        return best, mass, mean / mass

    pair_copy.wait_recv()
    best, mass, col_mean = join(col_pair, NC)
    col_stat[chip] = jnp.concatenate([best + jnp.log(mass), col_mean], axis=0)

    @pl.loop(1, CHIPS)
    def _(j):
        pltpu.make_async_remote_copy(
            src_ref=col_stat.at[chip], dst_ref=col_stat.at[chip],
            send_sem=stat_s.at[1], recv_sem=stat_r.at[1],
            device_id={"seq": lax.rem(chip + j, CHIPS) * NC + core}, device_id_type=MESH,
        ).start()

    row_all = row_stat.at[pl.ds(0, NZ - 1)]
    col_all = col_stat.at[pl.ds(0, CHIPS - 1)]
    pltpu.make_async_copy(row_all, row_all, stat_r.at[0]).wait()

    best, mass, row_mean = join(row_stat, NZ)
    row_scale = jnp.exp(row_max - best) / mass
    pltpu.make_async_copy(col_all, col_all, stat_r.at[1]).wait()
    best, mass, col_mean = join(col_stat, CHIPS)
    lines = lax.broadcasted_iota(jnp.int32, (EXP, EXP), 0)
    col_tile[...] = jnp.where(
        lines == 0, jnp.exp(col_top - best) / mass, jnp.where(lines == 1, col_mean, 0.0)
    ).T

    for n, rows in enumerate(blocks):
        combine = row_exp[rows, :] * row_scale
        dispatch = col_exp[rows, :] * col_tile[rows, 0:1]
        grad = combine * (cgrad[rows, :] - row_mean) + dispatch * (dgrad[rows, :] - col_tile[rows, 1:2])
        high = grad.astype(BF16)
        mat[rows, :] = (grad - high.astype(F32)).astype(BF16)
        mat[EXP + ROWS * n:EXP + ROWS * (n + 1), :] = high
        mat[2 * EXP + ROWS * n:2 * EXP + ROWS * (n + 1), :] = dispatch.astype(BF16)
        comb[rows, :] = combine.astype(BF16)
    fac[...] = mat[EXP:3 * EXP, :].T

    def term(d):
        stacked = params[...].reshape(2 * EXP, D)
        owner = lax.rem(z + d, NZ)
        part[d] = nn_dot(fac[pl.ds(pl.multiple_of(owner * OWN, OWN), OWN), :], stacked)

    ring = ({}, {})
    towards = ({"expert": lax.rem(z + 1, NZ)}, {"expert": lax.rem(z + NZ - 1, NZ)})

    def pass_on(way, i):
        d, h = (RIGHT, LEFT)[way][i]
        value = part[d if way == 0 else NZ - d, HALF * h:HALF * (h + 1), :]
        if (d + 1, h) in ring[way]:
            j, copy = ring[way][(d + 1, h)]
            copy.wait_recv()
            value = value + ring_in[way, j].astype(F32)
        stage[way, i] = value.astype(BF16)
        ring[way][(d, h)] = (
            i,
            send(stage.at[way, i], ring_in.at[way, i], ring_s.at[way, i], ring_r.at[way, i], towards[way]),
        )

    term(4)
    pass_on(0, 0)
    pass_on(1, 0)
    term(3)
    pass_on(0, 1)
    term(5)
    pass_on(1, 1)

    for n in range(D // 256):
        cols = slice(256 * n, 256 * (n + 1))
        pair = nn_dot(mat[0:2 * EXP, :], tok[:, cols])
        w_sum[:, cols] = pair[:EXP] + pair[EXP:]
        o_sum[:, cols] = nn_dot(comb[...], og[:, cols]).astype(BF16)
    there = pl.ds(pl.multiple_of((1 - core) * (EXP // 2), EXP // 2), EXP // 2)
    here = pl.ds(pl.multiple_of(core * (EXP // 2), EXP // 2), EXP // 2)
    core_w = send(w_sum.at[there], w_core, rc_s.at[0], rc_r.at[0], sibling)
    core_o = send(o_sum.at[there], o_core, rc_s.at[1], rc_r.at[1], sibling)
    for d in (2, 6, 1, 7, 0):
        term(d)

    pass_on(0, 2)
    pass_on(1, 2)

    core_w.wait_recv()
    core_o.wait_recv()
    w_mid[...] = (w_sum[here, :] + w_core[...]).reshape(NX, 16, D)
    o_mid[...] = (o_sum[here, :].astype(F32) + o_core[...].astype(F32)).astype(BF16).reshape(NX, 16, D)
    mid_sums = []
    for j in range(1, NX):
        to = lax.rem(x + j, NX)
        device = {"seq": seq_of(y, to)}
        mid_sums.append(send(w_mid.at[to], w_min.at[j - 1], rm_s.at[0, j - 1], rm_r.at[0, j - 1], device))
        mid_sums.append(send(o_mid.at[to], o_min.at[j - 1], rm_s.at[1, j - 1], rm_r.at[1, j - 1], device))

    pass_on(0, 3)
    pass_on(1, 3)
    pass_on(0, 4)
    pass_on(1, 4)

    pass_on(0, 5)
    pass_on(1, 5)

    for copy in mid_sums:
        copy.wait_recv()
    w16 = w_mid[x]
    o16 = o_mid[x].astype(F32)
    for j in range(NX - 1):
        w16 = w16 + w_min[j]
        o16 = o16 + o_min[j].astype(F32)
    for j in range(NY):
        w_end[j] = w16[4 * j:4 * j + 4]
        o_end[j] = o16[4 * j:4 * j + 4]
    slot = dp * NY + y
    w_ein[slot] = w_end[y]
    end_w, end_o = [], []
    for j in range(NY):
        to = lax.rem(y + j, NY)
        device = seq_of(to, x)
        end_w.append(
            send(w_end.at[to], w_ein.at[slot], re_s.at[0, j], re_r.at[0, j], {"dp": 1 - dp, "seq": device})
        )
        if j > 0:
            end_w.append(send(w_end.at[to], w_ein.at[slot], re_s.at[1, j], re_r.at[1, j], {"seq": device}))
            end_o.append(send(o_end.at[to], o_ein.at[j - 1], re_s.at[2, j], re_r.at[2, j], {"seq": device}))

    pass_on(0, 6)
    pass_on(1, 6)

    for copy in end_o:
        copy.wait_recv()
    total = o_end[y]
    for j in range(NY - 1):
        total = total + o_ein[j]
    so_ref[...] = total.astype(BF16)

    for copy in end_w:
        copy.wait_recv()
    total = w_ein[0]
    for j in range(1, 2 * NY):
        total = total + w_ein[j]
    sw_ref[...] = total

    for h in (1, 0):
        value = part[0, HALF * h:HALF * (h + 1), :]
        for way in range(2):
            j, copy = ring[way][(1, h)]
            copy.wait_recv()
            value = value + ring_in[way, j].astype(F32)
        tg_ref[HALF * h:HALF * (h + 1), :] = value.astype(BF16)

    for copy in pending:
        copy.wait_send()
    pltpu.make_async_copy(row_all, row_all, stat_s.at[0]).wait()
    pltpu.make_async_copy(col_all, col_all, stat_s.at[1]).wait()


def write_out(*refs):
    sems = refs[-1]
    copies = [pltpu.make_async_copy(refs[i], refs[3 + i], sems.at[i]) for i in range(3)]
    for copy in copies:
        copy.start()
    for copy in copies:
        copy.wait()


def on_device(tokens, slot_weight, slot_output, slot_input_grad, output_grad):
    vmem = pl.BlockSpec(memory_space=pltpu.VMEM)
    hbm = pl.BlockSpec(memory_space=pl.ANY)
    dma = pltpu.SemaphoreType.DMA
    shapes = (
        jax.ShapeDtypeStruct((OWN, D), BF16),
        jax.ShapeDtypeStruct((4, D), BF16),
        jax.ShapeDtypeStruct((4, D), F32),
    )
    results = pl.pallas_call(
        kernel,
        out_shape=tuple(pltpu.VMEM(shape.shape, shape.dtype) for shape in shapes),
        in_specs=[hbm] * 5,
        out_specs=(vmem, vmem, vmem),
        scratch_shapes=[
            pltpu.VMEM((TOK, D), BF16),
            pltpu.VMEM((TOK, D), BF16),
            pltpu.VMEM((3, 4, D), BF16),
            pltpu.VMEM((NY, 2, 4, D), BF16),
            pltpu.VMEM((NX, 4, D), BF16),
            pltpu.VMEM((2, NC, NX, 16, D), BF16),
            pltpu.VMEM((NC, NY, 16, D), BF16),
            pltpu.VMEM((EXP, TOK), F32),
            pltpu.VMEM((EXP, TOK), F32),
            pltpu.VMEM((EXP, TOK), F32),
            pltpu.VMEM((EXP, TOK), F32),
            pltpu.VMEM((EXP, TOK), F32),
            pltpu.VMEM((EXP, EXP), F32),
            pltpu.VMEM((NZ, 2, TOK), F32),
            pltpu.VMEM((CHIPS, 2, EXP), F32),
            pltpu.VMEM((NC, 2, EXP), F32),
            pltpu.VMEM((3 * EXP, TOK), BF16),
            pltpu.VMEM((EXP, TOK), BF16),
            pltpu.VMEM((TOK, 2 * EXP), BF16),
            pltpu.VMEM((NZ, OWN, D), F32),
            pltpu.VMEM((2, 7, HALF, D), BF16),
            pltpu.VMEM((2, 7, HALF, D), BF16),
            pltpu.VMEM((EXP, D), F32),
            pltpu.VMEM((EXP, D), BF16),
            pltpu.VMEM((EXP // 2, D), F32),
            pltpu.VMEM((EXP // 2, D), BF16),
            pltpu.VMEM((NX, 16, D), F32),
            pltpu.VMEM((NX, 16, D), BF16),
            pltpu.VMEM((NX - 1, 16, D), F32),
            pltpu.VMEM((NX - 1, 16, D), BF16),
            pltpu.VMEM((NY, 4, D), F32),
            pltpu.VMEM((NY, 4, D), F32),
            pltpu.VMEM((2 * NY, 4, D), F32),
            pltpu.VMEM((NY - 1, 4, D), F32),
            dma((5,)),
            dma((2, 3)), dma((2, 3)),
            dma((2, 3)), dma((2, 3)),
            dma((2, 4)), dma((2, 4)),
            dma((2,)), dma((2,)),
            dma(()), dma(()),
            dma((2, 7)), dma((2, 7)),
            dma((2,)), dma((2,)),
            dma((2, 3)), dma((2, 3)),
            dma((3, 4)), dma((3, 4)),
        ],
        compiler_params=pltpu.CompilerParams(
            collective_id=0, has_side_effects=True, vmem_limit_bytes=62 * 1024 * 1024 + 512 * 1024
        ),
        cost_estimate=pl.CostEstimate(
            flops=2_000_000_000, bytes_accessed=5_000_000, transcendentals=250_000
        ),
    )(tokens[0], slot_weight, slot_output[0], slot_input_grad[0], output_grad[0])
    token_grad, slot_output_grad, slot_weight_grad = pl.pallas_call(
        write_out,
        out_shape=shapes,
        in_specs=[vmem] * 3,
        out_specs=(hbm,) * 3,
        scratch_shapes=[dma((3,))],
    )(*[pltpu.with_memory_space_constraint(array, pltpu.VMEM) for array in results])
    return (token_grad[None], slot_output_grad[None], slot_weight_grad)


def solution(mesh):
    placed = (
        P("dp", "seq", None),
        P(("seq", "expert"), None),
        P("dp", ("seq", "expert"), None),
        P("dp", ("seq", "expert"), None),
        P("dp", "seq", None),
    )
    return jax.shard_map(
        on_device,
        mesh=mesh,
        in_specs=placed,
        out_specs=(
            P("dp", ("seq", "expert"), None),
            P("dp", ("seq", "expert"), None),
            P(("seq", "expert"), None),
        ),
        check_vma=False,
    )
```

```python
import jax
import jax.numpy as jnp
from jax import lax
from jax.experimental import pallas as pl
from jax.experimental.pallas import tpu as pltpu
from jax.sharding import PartitionSpec as P

F32 = jnp.float32
BF16 = jnp.bfloat16
MESH = pl.DeviceIdType.MESH

NY, NX, NC, NZ = 4, 4, 2, 8
CHIPS = NY * NX
D = 1280
TOK = 768
EXP = 128
OWN = TOK // NZ
HALF = OWN // 2
PART = 48
PARTS = HALF // PART

RIGHT = ((4, 0), (3, 1), (3, 0), (2, 1), (2, 0), (1, 1), (1, 0))
LEFT = ((4, 1), (3, 0), (3, 1), (2, 0), (2, 1), (1, 0), (1, 1))


def nt_dot(a, b):
    return lax.dot_general(a, b, (((1,), (1,)), ((), ())), preferred_element_type=F32)


def nn_dot(a, b):
    return jnp.dot(a, b, preferred_element_type=F32)


def kernel(
    tok_hbm, phi_hbm, out_hbm, inp_hbm, og_hbm,
    tg_ref, so_ref, sw_ref,
    tok, og, own, shard, shard_out, params, outs, logit, cgrad, dgrad, row_exp, col_exp, col_tile, row_stat, col_stat, col_pair,
    mat, comb, fac, part, stage, ring_in,
    w_sum, o_sum, w_core, o_core, w_mid, o_mid, w_min, o_min, w_end, o_end, w_ein, o_ein,
    load_sem, ys, yr, xs, xr, cs, cr, stat_s, stat_r, pair_s, pair_r, ring_s, ring_r, rc_s, rc_r, rm_s, rm_r, re_s, re_r,
):
    dp = lax.axis_index("dp")
    seq = lax.axis_index("seq")
    z = lax.axis_index("expert")
    core = lax.rem(seq, NC)
    x = lax.rem(seq // NC, NX)
    y = seq // (NC * NX)

    def seq_of(yy, xx):
        return (yy * NX + xx) * NC + core

    load_own = [
        pltpu.make_async_copy(src, own.at[t], load_sem.at[2 + t])
        for t, src in enumerate((phi_hbm, inp_hbm, out_hbm))
    ]
    for copy in load_own:
        copy.start()
    barrier = pltpu.get_barrier_semaphore()

    def greet(device):
        pl.semaphore_signal(barrier, inc=1, device_id=device, device_id_type=MESH)

    chip = y * NX + x
    sibling = {"seq": seq + 1 - 2 * core}
    greet(sibling)

    @pl.loop(1, CHIPS)
    def _(j):
        greet({"seq": lax.rem(chip + j, CHIPS) * NC + core})

    @pl.loop(1, NZ)
    def _(j):
        greet({"expert": lax.rem(z + j, NZ)})

    for j in range(NY):
        greet({"dp": 1 - dp, "seq": seq_of(lax.rem(y + j, NY), x)})

    load_tok = pltpu.make_async_copy(tok_hbm, tok, load_sem.at[0])
    load_og = pltpu.make_async_copy(og_hbm, og, load_sem.at[1])
    load_tok.start()
    load_og.start()
    for copy in load_own:
        copy.wait()
    pl.semaphore_wait(barrier, CHIPS + NZ - 1 + NY)

    pending = []

    def send(src, dst, s_sem, r_sem, device):
        copy = pltpu.make_async_remote_copy(
            src_ref=src, dst_ref=dst, send_sem=s_sem, recv_sem=r_sem,
            device_id=device, device_id_type=MESH,
        )
        copy.start()
        pending.append(copy)
        return copy

    pair_near, out_near, pair_far, out_far = [], [], [], []
    for j in range(1, NX):
        x_peer, y_peer = seq_of(y, lax.rem(x + j, NX)), seq_of(lax.rem(y + j, NY), x)
        out_near.append(
            send(own.at[2], shard_out.at[x], xs.at[0, j - 1], xr.at[0, j - 1], {"seq": x_peer})
        )
        pair_near.append(
            send(own.at[pl.ds(0, 2)], shard.at[y], ys.at[0, j - 1], yr.at[0, j - 1], {"seq": y_peer})
        )
    shard_out[x] = own[2]
    shard[y] = own[0:2]
    for copy in out_near:
        copy.wait_recv()
    rows = [shard_out[j].astype(F32) for j in range(NX)]
    outs[core, y] = jnp.concatenate(rows, axis=0).astype(BF16)
    own_out = outs.at[core, y]
    for j in range(1, NY):
        out_far.append(
            send(own_out, own_out, ys.at[1, j - 1], yr.at[1, j - 1], {"seq": seq_of(lax.rem(y + j, NY), x)})
        )
    for copy in pair_near:
        copy.wait_recv()
    for t in range(2):
        rows = [shard[j, t].astype(F32) for j in range(NY)]
        params[t, core, x] = jnp.concatenate(rows, axis=0).astype(BF16)
    own_pair = params.at[:, core, x]
    for j in range(1, NX):
        pair_far.append(
            send(own_pair, own_pair, xs.at[1, j - 1], xr.at[1, j - 1], {"seq": seq_of(y, lax.rem(x + j, NX))})
        )
    c_copies = [
        send(own_out, own_out, cs.at[1, 0], cr.at[1, 0], sibling),
        send(own_pair, own_pair, cs.at[0, 0], cr.at[0, 0], sibling),
    ]
    for j in (1, 3, 2):
        out_far[j - 1].wait_recv()
        block = outs.at[core, lax.rem(y - j + NY, NY)]
        c_copies.append(send(block, block, cs.at[1, j], cr.at[1, j], sibling))
        pair_far[j - 1].wait_recv()
        block = params.at[:, core, lax.rem(x - j + NX, NX)]
        c_copies.append(send(block, block, cs.at[0, j], cr.at[0, j], sibling))
    load_tok.wait()
    load_og.wait()
    for copy in c_copies:
        copy.wait_recv()

    both = params[...].reshape(2 * EXP, D)
    slot_outs = outs[...].reshape(EXP, D)
    for n in range(TOK // 256):
        cols = slice(256 * n, 256 * (n + 1))
        pair = nt_dot(both, tok[cols, :])
        logit[:, cols] = pair[:EXP]
        dgrad[:, cols] = pair[EXP:]
        swapped = nt_dot(slot_outs, og[cols, :])
        for c in range(NC):
            for yy in range(NY):
                for xx in range(NX):
                    put, get = (c * NX + xx) * 16 + 4 * yy, (c * NY + yy) * 16 + 4 * xx
                    cgrad[put:put + 4, cols] = swapped[get:get + 4]

    ROWS = 16
    blocks = [slice(ROWS * b, ROWS * (b + 1)) for b in range(EXP // ROWS)]
    lane = lax.broadcasted_iota(jnp.int32, (ROWS, EXP), 1)
    for rows in blocks:
        value = logit[rows, :]
        col_max = jnp.max(value, axis=1, keepdims=True)
        by_col = jnp.exp(value - col_max)
        col_exp[rows, :] = by_col
        col_sum = jnp.sum(by_col, axis=1, keepdims=True)
        col_dot = jnp.sum(by_col * dgrad[rows, :], axis=1, keepdims=True)
        col_tile[rows, :] = jnp.where(
            lane == 0,
            col_max + jnp.log(col_sum),
            jnp.where(lane == 1, col_dot / col_sum, jnp.where(lane == 2, col_max, 0.0)),
        )
    turned = col_tile[...].T
    col_pair[core] = turned[0:2, :]
    col_top = turned[2:3, :]
    pair_copy = send(col_pair.at[core], col_pair.at[core], pair_s, pair_r, sibling)
    top = logit[blocks[0], :]
    for rows in blocks[1:]:
        top = jnp.maximum(top, logit[rows, :])
    row_max = jnp.max(top, axis=0, keepdims=True)
    row_sum = jnp.zeros((ROWS, TOK), F32)
    row_dot = jnp.zeros((ROWS, TOK), F32)
    for rows in blocks:
        by_row = jnp.exp(logit[rows, :] - row_max)
        row_exp[rows, :] = by_row
        row_sum = row_sum + by_row
        row_dot = row_dot + by_row * cgrad[rows, :]
    row_sum = jnp.sum(row_sum, axis=0, keepdims=True)
    row_dot = jnp.sum(row_dot, axis=0, keepdims=True)
    row_stat[z] = jnp.concatenate([row_max + jnp.log(row_sum), row_dot / row_sum], axis=0)

    @pl.loop(1, NZ)
    def _(j):
        pltpu.make_async_remote_copy(
            src_ref=row_stat.at[z], dst_ref=row_stat.at[z],
            send_sem=stat_s.at[0], recv_sem=stat_r.at[0],
            device_id={"expert": lax.rem(z + j, NZ)}, device_id_type=MESH,
        ).start()

    def join(stat, count):
        best = stat[0][0:1]
        for j in range(1, count):
            best = jnp.maximum(best, stat[j][0:1])
        mass = jnp.zeros_like(best)
        mean = jnp.zeros_like(best)
        for j in range(count):
            one = stat[j]
            weight = jnp.exp(one[0:1] - best)
            mass = mass + weight
            mean = mean + weight * one[1:2]
        return best, mass, mean / mass

    pair_copy.wait_recv()
    best, mass, col_mean = join(col_pair, NC)
    col_stat[chip] = jnp.concatenate([best + jnp.log(mass), col_mean], axis=0)

    @pl.loop(1, CHIPS)
    def _(j):
        pltpu.make_async_remote_copy(
            src_ref=col_stat.at[chip], dst_ref=col_stat.at[chip],
            send_sem=stat_s.at[1], recv_sem=stat_r.at[1],
            device_id={"seq": lax.rem(chip + j, CHIPS) * NC + core}, device_id_type=MESH,
        ).start()

    row_all = row_stat.at[pl.ds(0, NZ - 1)]
    col_all = col_stat.at[pl.ds(0, CHIPS - 1)]
    pltpu.make_async_copy(row_all, row_all, stat_r.at[0]).wait()

    best, mass, row_mean = join(row_stat, NZ)
    row_scale = jnp.exp(row_max - best) / mass
    pltpu.make_async_copy(col_all, col_all, stat_r.at[1]).wait()
    best, mass, col_mean = join(col_stat, CHIPS)
    lines = lax.broadcasted_iota(jnp.int32, (EXP, EXP), 0)
    col_tile[...] = jnp.where(
        lines == 0, jnp.exp(col_top - best) / mass, jnp.where(lines == 1, col_mean, 0.0)
    ).T

    for n, rows in enumerate(blocks):
        combine = row_exp[rows, :] * row_scale
        dispatch = col_exp[rows, :] * col_tile[rows, 0:1]
        grad = combine * (cgrad[rows, :] - row_mean) + dispatch * (dgrad[rows, :] - col_tile[rows, 1:2])
        high = grad.astype(BF16)
        mat[rows, :] = (grad - high.astype(F32)).astype(BF16)
        mat[EXP + ROWS * n:EXP + ROWS * (n + 1), :] = high
        mat[2 * EXP + ROWS * n:2 * EXP + ROWS * (n + 1), :] = dispatch.astype(BF16)
        comb[rows, :] = combine.astype(BF16)
    fac[...] = mat[EXP:3 * EXP, :].T

    def term(d):
        stacked = params[...].reshape(2 * EXP, D)
        owner = lax.rem(z + d, NZ)
        part[d] = nn_dot(fac[pl.ds(pl.multiple_of(owner * OWN, OWN), OWN), :], stacked)

    ring = ({}, {})
    towards = ({"expert": lax.rem(z + 1, NZ)}, {"expert": lax.rem(z + NZ - 1, NZ)})

    def pass_on(way, i):
        d, h = (RIGHT, LEFT)[way][i]
        before = ring[way].get((d + 1, h))
        copies = []
        for q in range(PARTS):
            first = HALF * h + PART * q
            value = part[d if way == 0 else NZ - d, first:first + PART, :]
            if before is not None:
                before[1][q].wait_recv()
                value = value + ring_in[way, before[0], q].astype(F32)
            stage[way, i, q] = value.astype(BF16)
            copies.append(
                send(
                    stage.at[way, i, q], ring_in.at[way, i, q], ring_s.at[way, i, q], ring_r.at[way, i, q],
                    towards[way],
                )
            )
        ring[way][(d, h)] = (i, copies)

    term(4)
    pass_on(0, 0)
    pass_on(1, 0)
    term(3)
    pass_on(0, 1)
    term(5)
    pass_on(1, 1)

    for n in range(D // 256):
        cols = slice(256 * n, 256 * (n + 1))
        pair = nn_dot(mat[0:2 * EXP, :], tok[:, cols])
        w_sum[:, cols] = pair[:EXP] + pair[EXP:]
        o_sum[:, cols] = nn_dot(comb[...], og[:, cols]).astype(BF16)
    there = pl.ds(pl.multiple_of((1 - core) * (EXP // 2), EXP // 2), EXP // 2)
    here = pl.ds(pl.multiple_of(core * (EXP // 2), EXP // 2), EXP // 2)
    core_w = send(w_sum.at[there], w_core, rc_s.at[0], rc_r.at[0], sibling)
    core_o = send(o_sum.at[there], o_core, rc_s.at[1], rc_r.at[1], sibling)
    for d in (2, 6, 1, 7, 0):
        term(d)

    pass_on(0, 2)
    pass_on(1, 2)

    core_w.wait_recv()
    core_o.wait_recv()
    w_mid[...] = (w_sum[here, :] + w_core[...]).reshape(NX, 16, D)
    o_mid[...] = (o_sum[here, :].astype(F32) + o_core[...].astype(F32)).astype(BF16).reshape(NX, 16, D)
    mid_sums = []
    for j in range(1, NX):
        to = lax.rem(x + j, NX)
        device = {"seq": seq_of(y, to)}
        mid_sums.append(send(w_mid.at[to], w_min.at[j - 1], rm_s.at[0, j - 1], rm_r.at[0, j - 1], device))
        mid_sums.append(send(o_mid.at[to], o_min.at[j - 1], rm_s.at[1, j - 1], rm_r.at[1, j - 1], device))

    pass_on(0, 3)
    pass_on(1, 3)
    pass_on(0, 4)
    pass_on(1, 4)

    pass_on(0, 5)
    pass_on(1, 5)

    for copy in mid_sums:
        copy.wait_recv()
    w16 = w_mid[x]
    o16 = o_mid[x].astype(F32)
    for j in range(NX - 1):
        w16 = w16 + w_min[j]
        o16 = o16 + o_min[j].astype(F32)
    for j in range(NY):
        w_end[j] = w16[4 * j:4 * j + 4]
        o_end[j] = o16[4 * j:4 * j + 4]
    slot = dp * NY + y
    w_ein[slot] = w_end[y]
    end_w, end_o = [], []
    for j in range(NY):
        to = lax.rem(y + j, NY)
        device = seq_of(to, x)
        end_w.append(
            send(w_end.at[to], w_ein.at[slot], re_s.at[0, j], re_r.at[0, j], {"dp": 1 - dp, "seq": device})
        )
        if j > 0:
            end_w.append(send(w_end.at[to], w_ein.at[slot], re_s.at[1, j], re_r.at[1, j], {"seq": device}))
            end_o.append(send(o_end.at[to], o_ein.at[j - 1], re_s.at[2, j], re_r.at[2, j], {"seq": device}))

    pass_on(0, 6)
    pass_on(1, 6)

    for copy in end_o:
        copy.wait_recv()
    total = o_end[y]
    for j in range(NY - 1):
        total = total + o_ein[j]
    so_ref[...] = total.astype(BF16)

    for copy in end_w:
        copy.wait_recv()
    total = w_ein[0]
    for j in range(1, 2 * NY):
        total = total + w_ein[j]
    sw_ref[...] = total

    for h in (1, 0):
        for q in range(PARTS):
            first = HALF * h + PART * q
            value = part[0, first:first + PART, :]
            for way in range(2):
                i, copies = ring[way][(1, h)]
                copies[q].wait_recv()
                value = value + ring_in[way, i, q].astype(F32)
            tg_ref[first:first + PART, :] = value.astype(BF16)

    for copy in pending:
        copy.wait_send()
    pltpu.make_async_copy(row_all, row_all, stat_s.at[0]).wait()
    pltpu.make_async_copy(col_all, col_all, stat_s.at[1]).wait()


def write_out(*refs):
    sems = refs[-1]
    copies = [pltpu.make_async_copy(refs[i], refs[3 + i], sems.at[i]) for i in range(3)]
    for copy in copies:
        copy.start()
    for copy in copies:
        copy.wait()


def on_device(tokens, slot_weight, slot_output, slot_input_grad, output_grad):
    vmem = pl.BlockSpec(memory_space=pltpu.VMEM)
    hbm = pl.BlockSpec(memory_space=pl.ANY)
    dma = pltpu.SemaphoreType.DMA
    shapes = (
        jax.ShapeDtypeStruct((OWN, D), BF16),
        jax.ShapeDtypeStruct((4, D), BF16),
        jax.ShapeDtypeStruct((4, D), F32),
    )
    results = pl.pallas_call(
        kernel,
        out_shape=tuple(pltpu.VMEM(shape.shape, shape.dtype) for shape in shapes),
        in_specs=[hbm] * 5,
        out_specs=(vmem, vmem, vmem),
        scratch_shapes=[
            pltpu.VMEM((TOK, D), BF16),
            pltpu.VMEM((TOK, D), BF16),
            pltpu.VMEM((3, 4, D), BF16),
            pltpu.VMEM((NY, 2, 4, D), BF16),
            pltpu.VMEM((NX, 4, D), BF16),
            pltpu.VMEM((2, NC, NX, 16, D), BF16),
            pltpu.VMEM((NC, NY, 16, D), BF16),
            pltpu.VMEM((EXP, TOK), F32),
            pltpu.VMEM((EXP, TOK), F32),
            pltpu.VMEM((EXP, TOK), F32),
            pltpu.VMEM((EXP, TOK), F32),
            pltpu.VMEM((EXP, TOK), F32),
            pltpu.VMEM((EXP, EXP), F32),
            pltpu.VMEM((NZ, 2, TOK), F32),
            pltpu.VMEM((CHIPS, 2, EXP), F32),
            pltpu.VMEM((NC, 2, EXP), F32),
            pltpu.VMEM((3 * EXP, TOK), BF16),
            pltpu.VMEM((EXP, TOK), BF16),
            pltpu.VMEM((TOK, 2 * EXP), BF16),
            pltpu.VMEM((NZ, OWN, D), F32),
            pltpu.VMEM((2, 7, PARTS, PART, D), BF16),
            pltpu.VMEM((2, 7, PARTS, PART, D), BF16),
            pltpu.VMEM((EXP, D), F32),
            pltpu.VMEM((EXP, D), BF16),
            pltpu.VMEM((EXP // 2, D), F32),
            pltpu.VMEM((EXP // 2, D), BF16),
            pltpu.VMEM((NX, 16, D), F32),
            pltpu.VMEM((NX, 16, D), BF16),
            pltpu.VMEM((NX - 1, 16, D), F32),
            pltpu.VMEM((NX - 1, 16, D), BF16),
            pltpu.VMEM((NY, 4, D), F32),
            pltpu.VMEM((NY, 4, D), F32),
            pltpu.VMEM((2 * NY, 4, D), F32),
            pltpu.VMEM((NY - 1, 4, D), F32),
            dma((5,)),
            dma((2, 3)), dma((2, 3)),
            dma((2, 3)), dma((2, 3)),
            dma((2, 4)), dma((2, 4)),
            dma((2,)), dma((2,)),
            dma(()), dma(()),
            dma((2, 7, PARTS)), dma((2, 7, PARTS)),
            dma((2,)), dma((2,)),
            dma((2, 3)), dma((2, 3)),
            dma((3, 4)), dma((3, 4)),
        ],
        compiler_params=pltpu.CompilerParams(
            collective_id=0, has_side_effects=True, vmem_limit_bytes=62 * 1024 * 1024 + 512 * 1024
        ),
        cost_estimate=pl.CostEstimate(
            flops=2_000_000_000, bytes_accessed=5_000_000, transcendentals=250_000
        ),
    )(tokens[0], slot_weight, slot_output[0], slot_input_grad[0], output_grad[0])
    token_grad, slot_output_grad, slot_weight_grad = pl.pallas_call(
        write_out,
        out_shape=shapes,
        in_specs=[vmem] * 3,
        out_specs=(hbm,) * 3,
        scratch_shapes=[dma((3,))],
    )(*[pltpu.with_memory_space_constraint(array, pltpu.VMEM) for array in results])
    return (token_grad[None], slot_output_grad[None], slot_weight_grad)


def solution(mesh):
    placed = (
        P("dp", "seq", None),
        P(("seq", "expert"), None),
        P("dp", ("seq", "expert"), None),
        P("dp", ("seq", "expert"), None),
        P("dp", "seq", None),
    )
    return jax.shard_map(
        on_device,
        mesh=mesh,
        in_specs=placed,
        out_specs=(
            P("dp", ("seq", "expert"), None),
            P("dp", ("seq", "expert"), None),
            P(("seq", "expert"), None),
        ),
        check_vma=False,
    )
```
